256 devices in a mesh: atoms: 64 (over y, z, core), pair: 4 (over x).
Axes of the slice: x: 4, y: 4, z: 8, core: 2. Of those that a mesh axis runs over, the one named last changes fastest.
Arguments:
- trunk_single: bfloat16 [6144, 384], P('atoms'), may hold values from -6 to 6
- atom_feature: bfloat16 [49152, 128], P('atoms'), may hold values from -6 to 6
- pair_band: bfloat16 [6144, 256, 128], P('atoms'), may hold values from -6 to 6
- atom_token: int32 [49152], replicated, may hold values from 0 to 6143, as said below
- token_counts: int32 [6144], P('atoms'), may hold values from 1 to 24, as said below
- key_offsets: int32 [1536], P('atoms'), may hold values from -96 to 0
- single_weight: bfloat16 [384, 128], replicated, may hold values from -0.3125 to 0.3125
- attn_weight: bfloat16 [128, 4, 128], P(None, 'pair'), may hold values from -0.5 to 0.5
- bias_weight: float32 [128, 4], P(None, 'pair'), may hold values from -12 to 12
- out_weight: bfloat16 [128, 128], P('pair'), may hold values from -2 to 2
- token_weight: bfloat16 [128, 384], replicated, may hold values from -0.5 to 0.5
Outputs:
- atom_single: bfloat16 [49152, 128], P('atoms')
- token_single: bfloat16 [6144, 384], P('atoms')
The draws below stay inside these ranges and needn't reach their ends.
Inputs may be any that keep to these rules, and one draw needn't show every extreme that they name: Token i has token_counts[i] atoms. For every g, tokens g * 4 * 96 to (g + 1) * 4 * 96 - 1 have 4 * 768 atoms together. `atom_token`: never falls from one atom to the next; token i is named exactly token_counts[i] times, so atoms g * 4 * 768 to (g + 1) * 4 * 768 - 1 belong to tokens g * 4 * 96 to (g + 1) * 4 * 96 - 1.
All inputs are finite; a program needn't handle non-finite values.
Results may differ from the reference program's by a relative error of at most 0.02.
Values may be sent and summed in bfloat16 or wider, within the bound.
A program may use at most 128 MiB of HBM per device.

```python
import math
import jax
import jax.numpy as jnp
from jax import lax

CS = 384
CA = 128
CZ = 128
HEADS = 4
HD = 32
WQ = 32
WK = 128
GROUP = 4
MOST = 24
ATOM_DEV = 768
TOK_DEV = 96
REACH = 96
BAND = 256
NATOM = 49152
NTOK = 6144
NWIN = 1536


def token_layout(key):
    group_tokens = GROUP * TOK_DEV
    extra_most = MOST - 1
    groups = NTOK // group_tokens
    slot_total = group_tokens * extra_most
    ball_count = GROUP * ATOM_DEV - group_tokens - extra_most
    key_ligand, key_heavy, key_score = jax.random.split(key, 3)
    ligand_dev = jax.random.randint(key_ligand, (groups,), 0, GROUP, dtype=jnp.int32)
    heavy_spot = jax.random.randint(key_heavy, (groups,), 0, TOK_DEV, dtype=jnp.int32)
    heavy_token = (ligand_dev + 1) % GROUP * TOK_DEV + heavy_spot
    token_index = jnp.arange(group_tokens, dtype=jnp.int32)
    is_ligand = (token_index // TOK_DEV)[None, :] == ligand_dev[:, None]
    is_heavy = token_index[None, :] == heavy_token[:, None]
    slot_index = jnp.arange(slot_total, dtype=jnp.int32)
    slot_token = slot_index // extra_most
    blocked = (is_ligand | is_heavy)[:, slot_token]
    raw_scores = jax.random.randint(key_score, (groups, slot_total), 0, 2 ** 17, dtype=jnp.int32) * slot_total + slot_index[None, :]
    scores = jnp.where(blocked, -1 - slot_index[None, :], raw_scores)
    unused, picked = lax.top_k(scores, ball_count)
    picked_token = picked // extra_most
    gained = jnp.sum((picked_token[:, :, None] == token_index[None, None, :]).astype(jnp.int32), axis=1)
    counts = 1 + gained + jnp.where(is_heavy, extra_most, 0)
    token_ends = jnp.cumsum(counts, axis=1)
    atom_index = jnp.arange(GROUP * ATOM_DEV, dtype=jnp.int32)
    local_owner = jnp.sum((token_ends[:, None, :] <= atom_index[None, :, None]).astype(jnp.int32), axis=2)
    owners = local_owner + (jnp.arange(groups, dtype=jnp.int32) * group_tokens)[:, None]
    return (counts.reshape(NTOK).astype(jnp.int32), owners.reshape(NATOM).astype(jnp.int32))


def draw_token_counts(key, part):
    counts, owners = token_layout(key)
    return counts


def draw_atom_token(key, part):
    counts, owners = token_layout(key)
    return owners


def draw_bias_weight(key, part):
    key = jax.random.fold_in(key, 3)
    return jnp.clip(jax.random.normal(key, (CZ, HEADS), jnp.float32) * (2.0 / math.sqrt(CZ)), -12.0, 12.0)


def touch_ends(array, own_key, least, top_value):
    index_at = [jax.random.randint(jax.random.fold_in(own_key, axis), (), 0, length) for axis, length in enumerate(array.shape)]
    longest = array.shape.index(max(array.shape))
    neighbour = index_at[:longest] + [(index_at[longest] + 1) % array.shape[longest]] + index_at[longest + 1:]
    return array.at[tuple(index_at)].set(least).at[tuple(neighbour)].set(top_value)


def block_levels(stream_key, shape, pieces, low, high):
    def one(dim, shards_of):
        steps = jax.random.uniform(jax.random.fold_in(jax.random.fold_in(stream_key, 6), dim), (shards_of,), jnp.float32, low / len(pieces), high / len(pieces))
        return jnp.repeat(jnp.exp(steps), shape[dim] // shards_of).reshape((-1,) + (1,) * (len(shape) - dim - 1))

    gain = one(*pieces[0])
    for cut in pieces[1:]:
        gain = gain * one(*cut)
    return gain


def bell_draw(rng, shape, width, bound, cuts=(), held_as=jnp.bfloat16):
    entries = jax.random.normal(rng, shape, jnp.float32) * width
    if len(cuts) > 0:
        entries = block_levels(rng, shape, cuts, -0.22, 0.18) * entries
    return jnp.clip(entries, min=-bound, max=bound).astype(held_as)


def setup_inputs(seed: int = 0) -> dict:
    splits = jax.random.split(jax.random.key(seed), 12)
    return {
        "trunk_single": bell_draw(splits[0], (NTOK, CS), 1.0, 6.0, ((0, 64),)),
        "atom_feature": bell_draw(splits[1], (NATOM, CA), 1.0, 6.0, ((0, 64),)),
        "pair_band": bell_draw(splits[2], (NTOK, BAND, CZ), 1.0, 6.0, ((0, 64),)),
        "atom_token": draw_atom_token(jax.random.fold_in(splits[11], 71), 0),
        "token_counts": draw_token_counts(jax.random.fold_in(splits[11], 71), 0),
        "key_offsets": touch_ends(jax.random.randint(splits[5], (NWIN,), 0 - REACH, 1), jax.random.fold_in(splits[5], 1), 0 - REACH, 0).astype(jnp.int32),
        "single_weight": bell_draw(splits[6], (CS, CA), CS ** -0.5, 0.3125),
        "attn_weight": bell_draw(splits[7], (CA, HEADS, 4 * HD), CA ** -0.5, 0.5, ((1, 4),)),
        "bias_weight": draw_bias_weight(jax.random.fold_in(splits[11], 71), 0),
        "out_weight": bell_draw(splits[9], (HEADS * HD, CA), (HEADS * HD // 16) ** -0.5, 2.0, ((0, 4),)),
        "token_weight": bell_draw(splits[10], (CA, CS), CA ** -0.5, 0.5),
    }


def layer_norm(values):
    average = lax.optimization_barrier(jnp.mean(values, axis=-1, keepdims=True))
    centred = values - average
    spread = lax.optimization_barrier(jnp.mean(centred * centred, axis=-1, keepdims=True))
    return centred * lax.rsqrt(spread + 1e-05)

def reference(trunk_single, atom_feature, pair_band, atom_token, token_counts, key_offsets, single_weight, attn_weight, bias_weight, out_weight, token_weight):
    single_norm = layer_norm(trunk_single.astype(jnp.float32)).astype(jnp.bfloat16)
    token_proj = jnp.dot(single_norm, single_weight, preferred_element_type=jnp.float32).astype(jnp.bfloat16)
    atom_cond = (atom_feature.astype(jnp.float32) + token_proj[atom_token].astype(jnp.float32)).astype(jnp.bfloat16)
    cond_norm = layer_norm(atom_cond.astype(jnp.float32)).astype(jnp.bfloat16)
    projected = jnp.dot(cond_norm, attn_weight.reshape(CA, HEADS * 4 * HD), preferred_element_type=jnp.float32).astype(jnp.bfloat16)
    projected = projected.reshape(NATOM, HEADS, 4, HD)

    def band_block(block_rows):
        return jnp.einsum('icz,zh->ihc', layer_norm(block_rows.astype(jnp.float32)), bias_weight, precision=lax.Precision.HIGHEST)
    pair_bias = lax.map(band_block, pair_band.reshape(NTOK // TOK_DEV, TOK_DEV, BAND, CZ)).reshape(NTOK, HEADS, BAND)
    window_base = jnp.arange(NWIN, dtype=jnp.int32) * WQ
    query_pos = window_base[:, None] + jnp.arange(WQ, dtype=jnp.int32)[None, :]
    key_pos = (window_base + key_offsets)[:, None] + jnp.arange(WK, dtype=jnp.int32)[None, :]
    key_valid = (key_pos >= 0) & (key_pos < NATOM)
    key_clip = jnp.clip(key_pos, 0, NATOM - 1)
    query_tok = atom_token[query_pos]
    key_tok = atom_token[key_clip]
    band_index = jnp.clip(key_tok[:, None, :] - query_tok[:, :, None] + WK, 0, BAND - 1)
    head_range = jnp.arange(HEADS, dtype=jnp.int32)
    pair_term = pair_bias[query_tok[:, :, None, None], head_range[None, None, :, None], band_index[:, :, None, :]]
    own_rows = projected[query_pos]
    key_rows = projected[key_clip]
    scores = jnp.einsum('wqhd,wkhd->wqhk', own_rows[:, :, :, 0].astype(jnp.float32), key_rows[:, :, :, 1].astype(jnp.float32)) / math.sqrt(HD) + pair_term
    masked = jnp.where(key_valid[:, None, None, :], scores, -jnp.inf)
    row_top = lax.optimization_barrier(jnp.max(masked, axis=-1, keepdims=True))
    exponent = jnp.exp(masked - row_top)
    weights = (exponent / lax.optimization_barrier(jnp.sum(exponent, axis=-1, keepdims=True))).astype(jnp.bfloat16)
    attended = jnp.einsum('wqhk,wkhd->wqhd', weights.astype(jnp.float32), key_rows[:, :, :, 2].astype(jnp.float32))
    gated = (jax.nn.sigmoid(own_rows[:, :, :, 3].astype(jnp.float32)) * attended).astype(jnp.bfloat16)
    gated = gated.reshape(NATOM, HEADS * HD)
    update = jnp.dot(gated, out_weight, preferred_element_type=jnp.float32)
    atom_single = (atom_cond.astype(jnp.float32) + update).astype(jnp.bfloat16)
    per_atom = jax.nn.relu(jnp.dot(atom_single, token_weight, preferred_element_type=jnp.float32))
    token_sums = jax.ops.segment_sum(per_atom, atom_token, num_segments=NTOK)
    token_single = (token_sums / token_counts.astype(jnp.float32)[:, None]).astype(jnp.bfloat16)
    return (atom_single, token_single)
```

```python
import functools
import math

import jax
import jax.numpy as jnp
from jax import lax
from jax.experimental import pallas as pl
from jax.experimental.pallas import tpu as pltpu
from jax.sharding import PartitionSpec as P

GROUP = 4
LANES = 128
MESH = pl.DeviceIdType.MESH
F32 = jnp.float32
BF16 = jnp.bfloat16
CHUNKS = 4
NT = (((1,), (1,)), ((), ()))


def dot(a, b):
    return jnp.dot(a, b, preferred_element_type=F32)


def norm_rows(x):
    centred = x - jnp.mean(x, axis=-1, keepdims=True)
    spread = jnp.mean(centred * centred, axis=-1, keepdims=True)
    return centred * lax.rsqrt(spread + 1e-05)


def kernel(
    sizes,
    trunk, feat, band, tok, counts, koff, single_w, attn_w, bias_w, out_w, token_w,
    atom_out, token_out,
    band_v, tp_all, bias_all, cond, proj, qs, gate, onehot, onehot_t, tokq, tokl,
    ow_all, ow_cat, bias_hi, bias_lo, packed, atoms_bf, sums, sums_out, sums_in,
    band_sem, tp_send, tp_recv, ow_send, ow_recv, bias_send, bias_recv,
    halo_send, halo_recv, gate_send, gate_recv, sum_send, sum_recv,
):
    n_dev, n_pair, total_atoms = sizes
    tok_dev = trunk.shape[0]
    atom_dev = feat.shape[0]
    blocks = atom_dev // LANES
    reach = 96
    query_count = 32
    group_tok = GROUP * tok_dev
    part = tok_dev // CHUNKS
    a = lax.axis_index("atoms")
    p = lax.axis_index("pair")
    r = lax.rem(a, GROUP)
    base = a - r
    left = lax.rem(a + n_dev - 1, n_dev)
    right = lax.rem(a + 1, n_dev)

    def group_peer(d):
        return (base + lax.rem(r + d, GROUP), p)

    def pair_peer(d):
        return (a, lax.rem(p + d, n_pair))

    barrier = pltpu.get_barrier_semaphore()
    for d in range(1, GROUP):
        pl.semaphore_signal(barrier, inc=1, device_id=group_peer(d), device_id_type=MESH)
    for d in range(1, n_pair):
        pl.semaphore_signal(barrier, inc=1, device_id=pair_peer(d), device_id_type=MESH)
    pl.semaphore_signal(barrier, inc=1, device_id=(left, p), device_id_type=MESH)
    pl.semaphore_signal(barrier, inc=1, device_id=(right, p), device_id_type=MESH)

    def band_copy(c):
        rows = pl.ds(c * part, part)
        return pltpu.make_async_copy(band.at[rows], band_v.at[rows], band_sem.at[c])

    for c in range(CHUNKS):
        band_copy(c).start()

    def remote(src, dst, send, recv, device):
        return pltpu.make_async_remote_copy(
            src_ref=src, dst_ref=dst, send_sem=send, recv_sem=recv, device_id=device, device_id_type=MESH
        )

    def tp_copy(d):
        return remote(tp_all.at[r], tp_all.at[r], tp_send.at[d], tp_recv.at[d], group_peer(d))

    def tp_arrive(d):
        s = lax.rem(r + GROUP - d, GROUP)
        return remote(tp_all.at[s], tp_all.at[s], tp_send.at[d], tp_recv.at[d], group_peer(d))

    def ow_copy(d):
        return remote(ow_all.at[p], ow_all.at[p], ow_send.at[d], ow_recv.at[d], pair_peer(d))

    def ow_arrive(d):
        s = lax.rem(p + n_pair - d, n_pair)
        return remote(ow_all.at[s], ow_all.at[s], ow_send.at[d], ow_recv.at[d], pair_peer(d))

    def bias_copy(c, d):
        rows = pl.ds(c * part, part)
        return remote(
            bias_all.at[r, rows], bias_all.at[r, rows], bias_send.at[c, d], bias_recv.at[c, d], group_peer(d)
        )

    def bias_arrive(c, d):
        s = lax.rem(r + GROUP - d, GROUP)
        rows = pl.ds(c * part, part)
        return remote(
            bias_all.at[s, rows], bias_all.at[s, rows], bias_send.at[c, d], bias_recv.at[c, d], group_peer(d)
        )

    first, last = LANES, LANES + atom_dev

    def to_right():
        return remote(
            cond.at[pl.ds(last - reach, reach)], cond.at[pl.ds(first - reach, reach)],
            halo_send.at[0], halo_recv.at[0], (right, p),
        )

    def to_left():
        return remote(
            cond.at[pl.ds(first, reach)], cond.at[pl.ds(last, reach)],
            halo_send.at[1], halo_recv.at[1], (left, p),
        )

    def gate_copy(b, d):
        rows = pl.ds(b * query_count, query_count)
        return remote(
            packed.at[p, rows], packed.at[p, rows], gate_send.at[b, d], gate_recv.at[b, d], pair_peer(d)
        )

    def gate_arrive(b, d):
        s = lax.rem(p + n_pair - d, n_pair)
        rows = pl.ds(b * query_count, query_count)
        return remote(
            packed.at[s, rows], packed.at[s, rows], gate_send.at[b, d], gate_recv.at[b, d], pair_peer(d)
        )

    def sum_copy(d):
        t = lax.rem(r + d, GROUP)
        return remote(sums_out.at[t], sums_in.at[d], sum_send.at[d], sum_recv.at[d], group_peer(d))

    tp_all[r] = dot(norm_rows(trunk[...].astype(F32)).astype(BF16), single_w[...]).astype(BF16)
    ow_all[p] = out_w[...]
    for i in range(blocks + 2):
        row = lax.rem(a * blocks + i - 1 + total_atoms // LANES, total_atoms // LANES)
        tokl[i : i + 1, :] = tok[pl.ds(row, 1), :]

    pl.semaphore_wait(barrier, 3 + n_pair - 1 + 2)
    for d in range(1, GROUP):
        tp_copy(d).start()
    for d in range(1, n_pair):
        ow_copy(d).start()

    w = bias_w[...]
    w_hi = w.astype(BF16).astype(F32)
    w_mid = (w - w_hi).astype(BF16).astype(F32)
    w_lo = w - w_hi - w_mid
    w_total = jnp.sum(w, axis=1, keepdims=True)
    row_id = lax.broadcasted_iota(jnp.int32, (16, LANES), 0)
    parts = jnp.where(
        row_id == 0, w_hi, jnp.where(row_id == 1, w_mid, jnp.where(row_id == 2, w_lo, jnp.where(row_id == 3, 1.0, 0.0)))
    ).astype(BF16)
    lane8 = lax.broadcasted_iota(jnp.int32, (8, LANES), 1)
    diag_mask = lax.rem(lane8, 8) == lax.broadcasted_iota(jnp.int32, (8, LANES), 0)
    lane_group = lane8 // 8

    def band_rows(x):
        g = lax.dot_general(jnp.concatenate([x, parts], axis=0), x, NT, preferred_element_type=F32)
        acc = g[0:8]
        for s in range(1, LANES // 8):
            acc = jnp.where(lane_group == s, g[8 * s : 8 * s + 8], acc)
        squares = jnp.sum(jnp.where(diag_mask, acc, 0.0), axis=0, keepdims=True)
        products = g[LANES : LANES + 1] + g[LANES + 1 : LANES + 2] + g[LANES + 2 : LANES + 3]
        return products, g[LANES + 3 : LANES + 4], squares

    def band_step(start):
        halves = []
        for half in range(2):
            got = [band_rows(band_v[start + t, half * LANES : (half + 1) * LANES, :]) for t in range(8)]
            products, total, squares = (jnp.concatenate(list(v), axis=0) for v in zip(*got))
            mean = total * (1.0 / LANES)
            spread = jnp.maximum(squares * (1.0 / LANES) - mean * mean, 0.0)
            halves.append((products - mean * w_total) * lax.rsqrt(spread + 1e-05))
        bias_all[r, pl.ds(pl.multiple_of(start, 8), 8), :] = jnp.concatenate(halves, axis=1)

    def band_chunk(c, carry):
        band_copy(c).wait()

        def step(i, inner):
            band_step(c * part + i * 8)
            return inner

        lax.fori_loop(0, part // 8, step, 0)
        for d in range(1, GROUP):
            bias_copy(c, d).start()
        return carry

    lax.fori_loop(0, CHUNKS // 2, band_chunk, 0)

    token_base = (base * tok_dev).astype(jnp.int32)
    for d in range(1, GROUP):
        tp_arrive(d).wait_recv()
    cond[0 : first - reach, :] = jnp.zeros((first - reach, LANES), BF16)
    cond[last + reach : last + LANES, :] = jnp.zeros((LANES - reach, LANES), BF16)

    def cond_block(b, carry):
        rows = pl.ds(pl.multiple_of(b * LANES, LANES), LANES)
        tok_row = tokl[pl.ds(b + 1, 1), :] - token_base
        spread_row = jnp.broadcast_to(tok_row, (LANES, LANES))
        tok_col = spread_row.astype(F32).T.astype(jnp.int32)
        tokq[rows, :] = tok_col + token_base
        lane = lax.broadcasted_iota(jnp.int32, (LANES, LANES), 1)
        pick = jnp.concatenate(
            [(tok_col == lane + k * LANES).astype(F32).astype(BF16) for k in range(group_tok // LANES)], axis=1
        )
        onehot[rows, :] = pick
        sub = lax.broadcasted_iota(jnp.int32, (group_tok, LANES), 0)
        onehot_t[b] = (jnp.broadcast_to(tok_row, (group_tok, LANES)) == sub).astype(F32).astype(BF16)
        chosen = dot(pick, tp_all[...].reshape(group_tok, LANES)).astype(BF16)
        cond[pl.ds(pl.multiple_of(first + b * LANES, LANES), LANES), :] = (
            feat[rows, :].astype(F32) + chosen.astype(F32)
        ).astype(BF16)
        return carry

    lax.fori_loop(0, blocks, cond_block, 0)
    to_right().start()
    to_left().start()

    lax.fori_loop(CHUNKS // 2, CHUNKS, band_chunk, 0)

    lane1 = lax.broadcasted_iota(jnp.int32, (LANES, LANES), 1)
    aw = attn_w[...]
    aw32 = aw.astype(F32)
    head = lane1 // 32
    q_w = jnp.where(head == 1, pltpu.roll(aw32, 32, 1), 0.0).astype(BF16)
    g_w = jnp.where(head == 2, pltpu.roll(aw32, LANES - 32, 1), 0.0).astype(BF16)

    def proj_block(b, carry):
        rows = pl.ds(pl.multiple_of(b * LANES, LANES), LANES)
        ext = pl.ds(pl.multiple_of(first + b * LANES, LANES), LANES)
        normed = norm_rows(cond[ext, :].astype(F32)).astype(BF16)
        proj[ext, :] = dot(normed, aw).astype(BF16)
        qs[rows, :] = dot(normed, q_w).astype(BF16)
        gate[rows, :] = jax.nn.sigmoid(dot(normed, g_w).astype(BF16).astype(F32))
        return carry

    lax.fori_loop(0, blocks, proj_block, 0)
    to_right().wait_recv()
    to_left().wait_recv()
    for start in (0, last):
        normed = norm_rows(cond[start : start + LANES, :].astype(F32)).astype(BF16)
        proj[start : start + LANES, :] = dot(normed, aw).astype(BF16)

    for d in range(1, n_pair):
        ow_arrive(d).wait_recv()
    ow_cat[...] = jnp.zeros(ow_cat.shape, BF16)
    for h in range(n_pair):
        for j in range(4):
            ow_cat[h * LANES + 32 * j : h * LANES + 32 * j + 32, j * LANES : (j + 1) * LANES] = ow_all[h]

    def wait_bias(c, carry):
        for d in range(1, GROUP):
            bias_arrive(c, d).wait_recv()
        return carry

    lax.fori_loop(0, CHUNKS, wait_bias, 0)
    for s in range(GROUP):
        whole = bias_all[s]
        high = whole.astype(BF16)
        bias_hi[s] = high
        bias_lo[s] = (whole - high.astype(F32)).astype(BF16)

    width = 3 * LANES

    def attend(b, carry):
        rows = pl.ds(pl.multiple_of(b * LANES, LANES), LANES)
        keys = proj[pl.ds(pl.multiple_of(b * LANES, LANES), width), :]
        raw = lax.dot_general(qs[rows, :], keys, NT, preferred_element_type=F32) * (1.0 / math.sqrt(32.0))
        pick = onehot[rows, :]
        mine = dot(pick, bias_hi[...].reshape(group_tok, 2 * LANES)) + dot(
            pick, bias_lo[...].reshape(group_tok, 2 * LANES)
        )
        low, high = mine[:, :LANES], mine[:, LANES:]
        my_tok = tokq[rows, :]
        sub = lax.broadcasted_iota(jnp.int32, (LANES, LANES), 0)
        window = sub // query_count
        offset = jnp.where(
            window == 0,
            koff[4 * b],
            jnp.where(window == 1, koff[4 * b + 1], jnp.where(window == 2, koff[4 * b + 2], koff[4 * b + 3])),
        )
        shift = offset + window * query_count
        pieces = []
        for t in range(3):
            index = tokl[pl.ds(b + t, 1), :] - my_tok + LANES
            wrapped = index & (LANES - 1)
            first_half = jnp.take_along_axis(low, wrapped, axis=1, mode="promise_in_bounds")
            second_half = jnp.take_along_axis(high, wrapped, axis=1, mode="promise_in_bounds")
            value = raw[:, t * LANES : (t + 1) * LANES] + jnp.where(index >= LANES, second_half, first_half)
            slot = lane1 + (t - 1) * LANES - shift
            place = lane1 + (a * atom_dev + (b + t - 1) * LANES)
            valid = (slot >= 0) & (slot < LANES) & (place >= 0) & (place < total_atoms)
            pieces.append(jnp.where(valid, value, -jnp.inf))
        masked = jnp.concatenate(pieces, axis=1)
        top = jnp.max(masked, axis=1, keepdims=True)
        exponent = jnp.exp(masked - top)
        weights = (exponent / jnp.sum(exponent, axis=1, keepdims=True)).astype(BF16)
        gated = gate[rows, :] * dot(weights, keys)
        lane32 = lax.broadcasted_iota(jnp.int32, (query_count, LANES), 1) // 32
        out = jnp.zeros((query_count, LANES), F32)
        for j in range(4):
            turned = pltpu.roll(gated[32 * j : 32 * j + 32], (32 * j + 64) % LANES, 1)
            out = jnp.where(lane32 == j, turned, out)
        packed[p, pl.ds(pl.multiple_of(b * query_count, 32), query_count), :] = out.astype(BF16)
        for d in range(1, n_pair):
            gate_copy(b, d).start()
        return carry

    lax.fori_loop(0, blocks, attend, 0)

    def wait_gate(b, carry):
        for d in range(1, n_pair):
            gate_arrive(b, d).wait_recv()
        return carry

    lax.fori_loop(0, blocks, wait_gate, 0)

    update = dot(packed[0], ow_cat[0:LANES, :])
    for h in range(1, n_pair):
        update = update + dot(packed[h], ow_cat[h * LANES : (h + 1) * LANES, :])
    for b in range(blocks):
        for j in range(4):
            at = b * LANES + 32 * j
            value = cond[first + at : first + at + 32, :].astype(F32) + update[
                32 * b : 32 * b + 32, j * LANES : (j + 1) * LANES
            ]
            atoms_bf[at : at + 32, :] = value.astype(BF16)
    atom_out[...] = atoms_bf[...]
    total = None
    for b in range(blocks):
        per_atom = jnp.maximum(dot(atoms_bf[b * LANES : (b + 1) * LANES, :], token_w[...]), 0.0).astype(BF16)
        term = dot(onehot_t[b], per_atom)
        total = term if total is None else total + term
    for s in range(GROUP):
        sums[s] = total[s * tok_dev : (s + 1) * tok_dev]
        sums_out[s] = total[s * tok_dev : (s + 1) * tok_dev].astype(BF16)
    for d in range(1, GROUP):
        sum_copy(d).start()
    eye = lax.broadcasted_iota(jnp.int32, (tok_dev, tok_dev), 0) == lax.broadcasted_iota(
        jnp.int32, (tok_dev, tok_dev), 1
    )
    count = jnp.sum(jnp.where(eye, counts[...].astype(F32), 0.0), axis=1, keepdims=True)
    result = sums[r]
    for d in range(1, GROUP):
        sum_copy(d).wait_recv()
        result = result + sums_in[d].astype(F32)
    token_out[...] = (result / count).astype(BF16)

    for d in range(1, GROUP):
        tp_copy(d).wait_send()
        sum_copy(d).wait_send()
    for d in range(1, n_pair):
        ow_copy(d).wait_send()
    to_right().wait_send()
    to_left().wait_send()

    def drain_bias(c, carry):
        for d in range(1, GROUP):
            bias_copy(c, d).wait_send()
        return carry

    lax.fori_loop(0, CHUNKS, drain_bias, 0)

    def drain_gate(b, carry):
        for d in range(1, n_pair):
            gate_copy(b, d).wait_send()
        return carry

    lax.fori_loop(0, blocks, drain_gate, 0)


def shards(
    trunk_single, atom_feature, pair_band, atom_token, token_counts, key_offsets,
    single_weight, attn_weight, bias_weight, out_weight, token_weight,
):
    n_dev = lax.axis_size("atoms")
    n_pair = lax.axis_size("pair")
    tok_dev, width = trunk_single.shape
    atom_dev = atom_feature.shape[0]
    blocks = atom_dev // LANES
    total_atoms = atom_token.shape[0]
    group_tok = GROUP * tok_dev
    ext = atom_dev + 2 * LANES
    vmem = pl.BlockSpec(memory_space=pltpu.VMEM)
    dma = pltpu.SemaphoreType.DMA
    return pl.pallas_call(
        functools.partial(kernel, (n_dev, n_pair, total_atoms)),
        out_shape=(
            jax.ShapeDtypeStruct((atom_dev, LANES), BF16),
            jax.ShapeDtypeStruct((tok_dev, width), BF16),
        ),
        in_specs=[
            vmem, vmem, pl.BlockSpec(memory_space=pl.ANY), vmem, vmem,
            pl.BlockSpec(memory_space=pltpu.SMEM), vmem, vmem, vmem, vmem, vmem,
        ],
        out_specs=(vmem, vmem),
        scratch_shapes=[
            pltpu.VMEM(pair_band.shape, BF16),
            pltpu.VMEM((GROUP, tok_dev, LANES), BF16),
            pltpu.VMEM((GROUP, tok_dev, 2 * LANES), F32),
            pltpu.VMEM((ext, LANES), BF16),
            pltpu.VMEM((ext, LANES), BF16),
            pltpu.VMEM((atom_dev, LANES), BF16),
            pltpu.VMEM((atom_dev, LANES), F32),
            pltpu.VMEM((atom_dev, group_tok), BF16),
            pltpu.VMEM((blocks, group_tok, LANES), BF16),
            pltpu.VMEM((atom_dev, LANES), jnp.int32),
            pltpu.VMEM((blocks + 2, LANES), jnp.int32),
            pltpu.VMEM((n_pair, 32, LANES), BF16),
            pltpu.VMEM((n_pair * LANES, 4 * LANES), BF16),
            pltpu.VMEM((GROUP, tok_dev, 2 * LANES), BF16),
            pltpu.VMEM((GROUP, tok_dev, 2 * LANES), BF16),
            pltpu.VMEM((n_pair, atom_dev // 4, LANES), BF16),
            pltpu.VMEM((atom_dev, LANES), BF16),
            pltpu.VMEM((GROUP, tok_dev, width), F32),
            pltpu.VMEM((GROUP, tok_dev, width), BF16),
            pltpu.VMEM((GROUP, tok_dev, width), BF16),
            dma((CHUNKS,)),
            dma((GROUP,)), dma((GROUP,)),
            dma((n_pair,)), dma((n_pair,)),
            dma((CHUNKS, GROUP)), dma((CHUNKS, GROUP)),
            dma((2,)), dma((2,)),
            dma((blocks, n_pair)), dma((blocks, n_pair)),
            dma((GROUP,)), dma((GROUP,)),
        ],
        compiler_params=pltpu.CompilerParams(
            collective_id=0, has_side_effects=True, vmem_limit_bytes=48 * 1024 * 1024
        ),
        name="encoder",
    )(
        trunk_single,
        atom_feature,
        pair_band,
        atom_token.reshape(total_atoms // LANES, LANES),
        token_counts.reshape(1, tok_dev),
        key_offsets,
        single_weight,
        attn_weight.reshape(attn_weight.shape[0], attn_weight.shape[2]),
        bias_weight.reshape(1, bias_weight.shape[0]),
        out_weight,
        token_weight,
    )


def solution(mesh):
    placed = (
        P("atoms", None),
        P("atoms", None),
        P("atoms", None, None),
        P(),
        P("atoms"),
        P("atoms"),
        P(),
        P(None, "pair", None),
        P(None, "pair"),
        P("pair", None),
        P(),
    )
    return jax.shard_map(
        shards,
        mesh=mesh,
        in_specs=placed,
        out_specs=(P("atoms", None), P("atoms", None)),
        check_vma=False,
    )
```

```python
import functools
import math

import jax
import jax.numpy as jnp
from jax import lax
from jax.experimental import pallas as pl
from jax.experimental.pallas import tpu as pltpu
from jax.sharding import PartitionSpec as P

GROUP = 4
LANES = 128
MESH = pl.DeviceIdType.MESH
F32 = jnp.float32
BF16 = jnp.bfloat16
CHUNKS = 4
UA, UB, UC = 24, 6, 6
NT = (((1,), (1,)), ((), ()))


def dot(a, b):
    return jnp.dot(a, b, preferred_element_type=F32)


def norm_rows(x):
    centred = x - jnp.mean(x, axis=-1, keepdims=True)
    spread = jnp.mean(centred * centred, axis=-1, keepdims=True)
    return centred * lax.rsqrt(spread + 1e-05)


def kernel(
    sizes,
    trunk_h, feat_h, band, tok_h, counts_h, koff_h, single_h, attn_h, bias_h, out_h, token_h,
    atom_out, token_out,
    trunk, feat, tok, counts, koff, single_w, attn_w, bias_w, token_w, in_sem,
    band_v, tp_all, bias_all, cond, keys, queries, gate, onehot, onehot_t, tok_info, tokl, mine,
    scores, weights, window_keys,
    ow_all, ow_cat, bias_hi, bias_lo, packed, atoms_bf, sums, sums_out, sums_in,
    band_sem, tp_send, tp_recv, ow_send, ow_recv, bias_send, bias_recv,
    halo_send, halo_recv, gate_send, gate_recv, sum_send, sum_recv,
):
    n_dev, n_pair, total_atoms = sizes
    tok_dev = trunk.shape[0]
    atom_dev = feat.shape[0]
    blocks = atom_dev // LANES
    reach = 96
    query_count = 32
    group_tok = GROUP * tok_dev
    part = tok_dev // CHUNKS
    a = lax.axis_index("atoms")
    p = lax.axis_index("pair")
    r = lax.rem(a, GROUP)
    base = a - r
    left = lax.rem(a + n_dev - 1, n_dev)
    right = lax.rem(a + 1, n_dev)

    def group_peer(d):
        return (base + lax.rem(r + d, GROUP), p)

    def pair_peer(d):
        return (a, lax.rem(p + d, n_pair))

    barrier = pltpu.get_barrier_semaphore()
    for d in range(1, GROUP):
        pl.semaphore_signal(barrier, inc=1, device_id=group_peer(d), device_id_type=MESH)
    for d in range(1, n_pair):
        pl.semaphore_signal(barrier, inc=1, device_id=pair_peer(d), device_id_type=MESH)
    pl.semaphore_signal(barrier, inc=1, device_id=(left, p), device_id_type=MESH)
    pl.semaphore_signal(barrier, inc=1, device_id=(right, p), device_id_type=MESH)

    def band_copy(c):
        rows = pl.ds(c * part, part)
        return pltpu.make_async_copy(band.at[rows], band_v.at[rows], band_sem.at[c])

    loads = [
        pltpu.make_async_copy(src, dst, in_sem.at[i])
        for i, (src, dst) in enumerate(
            (
                (trunk_h, trunk), (single_h, single_w), (out_h, ow_all.at[p]), (bias_h, bias_w), (tok_h, tok),
                (feat_h, feat), (attn_h, attn_w), (koff_h, koff), (token_h, token_w), (counts_h, counts),
            )
        )
    ]
    for load in loads[:4]:
        load.start()
    band_copy(0).start()
    for load in loads[4:]:
        load.start()
    for c in range(1, CHUNKS):
        band_copy(c).start()

    def remote(src, dst, send, recv, device):
        return pltpu.make_async_remote_copy(
            src_ref=src, dst_ref=dst, send_sem=send, recv_sem=recv, device_id=device, device_id_type=MESH
        )

    def tp_copy(d):
        return remote(tp_all.at[r], tp_all.at[r], tp_send.at[d], tp_recv.at[d], group_peer(d))

    def tp_arrive(d):
        s = lax.rem(r + GROUP - d, GROUP)
        return remote(tp_all.at[s], tp_all.at[s], tp_send.at[d], tp_recv.at[d], group_peer(d))

    def ow_copy(d):
        return remote(ow_all.at[p], ow_all.at[p], ow_send.at[d], ow_recv.at[d], pair_peer(d))

    def ow_arrive(d):
        s = lax.rem(p + n_pair - d, n_pair)
        return remote(ow_all.at[s], ow_all.at[s], ow_send.at[d], ow_recv.at[d], pair_peer(d))

    def bias_copy(c, d):
        rows = pl.ds(c * part, part)
        return remote(
            bias_all.at[r, rows], bias_all.at[r, rows], bias_send.at[c, d], bias_recv.at[c, d], group_peer(d)
        )

    def bias_arrive(c, d):
        s = lax.rem(r + GROUP - d, GROUP)
        rows = pl.ds(c * part, part)
        return remote(
            bias_all.at[s, rows], bias_all.at[s, rows], bias_send.at[c, d], bias_recv.at[c, d], group_peer(d)
        )

    first, last = LANES, LANES + atom_dev

    def to_right():
        return remote(
            cond.at[pl.ds(last - reach, reach)], cond.at[pl.ds(first - reach, reach)],
            halo_send.at[0], halo_recv.at[0], (right, p),
        )

    def to_left():
        return remote(
            cond.at[pl.ds(first, reach)], cond.at[pl.ds(last, reach)],
            halo_send.at[1], halo_recv.at[1], (left, p),
        )

    def gate_copy(b, d):
        rows = pl.ds(b * query_count, query_count)
        return remote(
            packed.at[p, rows], packed.at[p, rows], gate_send.at[b, d], gate_recv.at[b, d], pair_peer(d)
        )

    def gate_arrive(b, d):
        s = lax.rem(p + n_pair - d, n_pair)
        rows = pl.ds(b * query_count, query_count)
        return remote(
            packed.at[s, rows], packed.at[s, rows], gate_send.at[b, d], gate_recv.at[b, d], pair_peer(d)
        )

    def sum_copy(d):
        t = lax.rem(r + d, GROUP)
        return remote(sums_out.at[t], sums_in.at[d], sum_send.at[d], sum_recv.at[d], group_peer(d))

    for load in loads[:3]:
        load.wait()
    tp_all[r] = dot(norm_rows(trunk[...].astype(F32)).astype(BF16), single_w[...]).astype(BF16)
    pl.semaphore_wait(barrier, 3 + n_pair - 1 + 2)
    for d in range(1, GROUP):
        tp_copy(d).start()
    for d in range(1, n_pair):
        ow_copy(d).start()

    loads[3].wait()
    w = bias_w[...]
    w_hi = w.astype(BF16).astype(F32)
    w_mid = (w - w_hi).astype(BF16).astype(F32)
    w_lo = w - w_hi - w_mid
    w_total = jnp.sum(w, axis=1, keepdims=True)
    row_id = lax.broadcasted_iota(jnp.int32, (16, LANES), 0)
    parts = jnp.where(
        row_id == 0, w_hi, jnp.where(row_id == 1, w_mid, jnp.where(row_id == 2, w_lo, jnp.where(row_id == 3, 1.0, 0.0)))
    ).astype(BF16)
    lane8 = lax.broadcasted_iota(jnp.int32, (8, LANES), 1)
    diag_mask = lax.rem(lane8, 8) == lax.broadcasted_iota(jnp.int32, (8, LANES), 0)
    lane_group = lane8 // 8

    def band_rows(x):
        g = lax.dot_general(jnp.concatenate([x, parts], axis=0), x, NT, preferred_element_type=F32)
        acc = g[0:8]
        for s in range(1, LANES // 8):
            acc = jnp.where(lane_group == s, g[8 * s : 8 * s + 8], acc)
        squares = jnp.sum(jnp.where(diag_mask, acc, 0.0), axis=0, keepdims=True)
        products = g[LANES : LANES + 1] + g[LANES + 1 : LANES + 2] + g[LANES + 2 : LANES + 3]
        return products, g[LANES + 3 : LANES + 4], squares

    def band_step(start):
        halves = []
        for half in range(2):
            got = [band_rows(band_v[start + t, half * LANES : (half + 1) * LANES, :]) for t in range(8)]
            products, total, squares = (jnp.concatenate(list(v), axis=0) for v in zip(*got))
            mean = total * (1.0 / LANES)
            spread = jnp.maximum(squares * (1.0 / LANES) - mean * mean, 0.0)
            halves.append((products - mean * w_total) * lax.rsqrt(spread + 1e-05))
        bias_all[r, pl.ds(pl.multiple_of(start, 8), 8), :] = jnp.concatenate(halves, axis=1)

    def band_chunk(c, carry):
        band_copy(c).wait()

        def step(i, inner):
            band_step(c * part + i * 8)
            return inner

        lax.fori_loop(0, part // 8, step, 0, unroll=True)
        for d in range(1, GROUP):
            bias_copy(c, d).start()
        return carry

    lax.fori_loop(0, CHUNKS // 2, band_chunk, 0)

    for load in loads[4:]:
        load.wait()
    for i in range(blocks + 2):
        row = lax.rem(a * blocks + i - 1 + total_atoms // LANES, total_atoms // LANES)
        tokl[i : i + 1, :] = tok[pl.ds(row, 1), :]
    token_base = (base * tok_dev).astype(jnp.int32)
    for d in range(1, GROUP):
        tp_arrive(d).wait_recv()
    cond[0 : first - reach, :] = jnp.zeros((first - reach, LANES), BF16)
    cond[last + reach : last + LANES, :] = jnp.zeros((LANES - reach, LANES), BF16)

    lane1 = lax.broadcasted_iota(jnp.int32, (LANES, LANES), 1)

    def info_block(i, carry):
        tok_row = tokl[pl.ds(i, 1), :] - token_base
        spread_row = jnp.broadcast_to(tok_row, (LANES, LANES))
        tok_info[i] = spread_row.astype(F32).T.astype(jnp.int32)
        return carry

    lax.fori_loop(0, blocks + 2, info_block, 0, unroll=True)

    def cond_block(b, carry):
        rows = pl.ds(pl.multiple_of(b * LANES, LANES), LANES)
        tok_row = tokl[pl.ds(b + 1, 1), :] - token_base
        tok_col = tok_info[b + 1]
        pick = jnp.concatenate(
            [(tok_col == lane1 + k * LANES).astype(F32).astype(BF16) for k in range(group_tok // LANES)], axis=1
        )
        onehot[rows, :] = pick
        sub = lax.broadcasted_iota(jnp.int32, (group_tok, LANES), 0)
        onehot_t[b] = (jnp.broadcast_to(tok_row, (group_tok, LANES)) == sub).astype(F32).astype(BF16)
        chosen = dot(pick, tp_all[...].reshape(group_tok, LANES)).astype(BF16)
        cond[pl.ds(pl.multiple_of(first + b * LANES, LANES), LANES), :] = (
            feat[rows, :].astype(F32) + chosen.astype(F32)
        ).astype(BF16)
        return carry

    lax.fori_loop(0, blocks, cond_block, 0, unroll=True)
    to_right().start()
    to_left().start()

    lax.fori_loop(CHUNKS // 2, CHUNKS, band_chunk, 0)

    aw = attn_w[...]
    aw32 = aw.astype(F32)
    head = lane1 // 32
    q_w = jnp.where(head == 1, pltpu.roll(aw32, 32, 1), 0.0).astype(BF16)
    g_w = jnp.where(head == 2, pltpu.roll(aw32, LANES - 32, 1), 0.0).astype(BF16)
    kv_lane = (head == 1) | (head == 2)

    def key_rows(i, normed):
        place = lax.broadcasted_iota(jnp.int32, (LANES, LANES), 0) + (a * atom_dev + (i - 1) * LANES)
        absent = jnp.where((place >= 0) & (place < total_atoms), 0.0, -1e30)
        token = tok_info[i] + LANES
        info = jnp.where(
            lane1 == 0,
            (token >> 4).astype(F32),
            jnp.where(lane1 == 1, (token & 15).astype(F32), jnp.where(lane1 == 3, absent, jnp.where((lane1 == 2) | (lane1 == 4), 1.0, 0.0))),
        )
        keys[pl.ds(pl.multiple_of(i * LANES, LANES), LANES), :] = jnp.where(
            kv_lane, dot(normed, aw).astype(BF16).astype(F32), info
        )

    def proj_block(b, carry):
        rows = pl.ds(pl.multiple_of(b * LANES, LANES), LANES)
        normed = norm_rows(cond[pl.ds(pl.multiple_of(first + b * LANES, LANES), LANES), :].astype(F32)).astype(BF16)
        key_rows(b + 1, normed)
        query = jnp.where(lane1 == 3, 1.0, dot(normed, q_w)).astype(BF16)
        token = tok_info[b + 1] + LANES
        against = jnp.where(
            lane1 == 0,
            16.0,
            jnp.where(
                lane1 == 1,
                1.0,
                jnp.where(
                    lane1 == 2,
                    (LANES - (token >> 4) * 16).astype(F32),
                    jnp.where(lane1 == 4, (-(token & 15)).astype(F32), 0.0),
                ),
            ),
        ).astype(BF16)
        for j in range(4):
            queries[4 * b + j, 0:32, :] = query[32 * j : 32 * j + 32]
            queries[4 * b + j, 32:64, :] = against[32 * j : 32 * j + 32]
        gate[rows, :] = jax.nn.sigmoid(dot(normed, g_w).astype(BF16).astype(F32))
        return carry

    lax.fori_loop(0, blocks, proj_block, 0, unroll=True)
    to_right().wait_recv()
    to_left().wait_recv()
    for i in (0, blocks + 1):
        key_rows(i, norm_rows(cond[i * LANES : (i + 1) * LANES, :].astype(F32)).astype(BF16))

    for d in range(1, n_pair):
        ow_arrive(d).wait_recv()
    ow_cat[...] = jnp.zeros(ow_cat.shape, BF16)
    for h in range(n_pair):
        for j in range(4):
            ow_cat[h * LANES + 32 * j : h * LANES + 32 * j + 32, j * LANES : (j + 1) * LANES] = ow_all[h]

    def wait_bias(c, carry):
        for d in range(1, GROUP):
            bias_arrive(c, d).wait_recv()
        return carry

    lax.fori_loop(0, CHUNKS, wait_bias, 0)
    for s in range(GROUP):
        whole = bias_all[s]
        high = whole.astype(BF16)
        bias_hi[s] = high
        bias_lo[s] = (whole - high.astype(F32)).astype(BF16)

    mine[...] = dot(onehot[...], bias_hi[...].reshape(group_tok, 2 * LANES)) + dot(
        onehot[...], bias_lo[...].reshape(group_tok, 2 * LANES)
    )

    lane32 = lax.broadcasted_iota(jnp.int32, (query_count, LANES), 1) // 32
    windows = atom_dev // query_count

    def score(w, carry):
        start = LANES + query_count * w + koff[w]
        window = keys[pl.ds(start, LANES), :].astype(BF16)
        window_keys[w] = window
        scores[w] = lax.dot_general(queries[w], window, NT, preferred_element_type=F32)
        return carry

    lax.fori_loop(0, windows, score, 0, unroll=UA)

    def soften(b, carry):
        rows = pl.ds(pl.multiple_of(b * LANES, LANES), LANES)
        raw = scores[pl.ds(4 * b, 4)]
        index = raw[:, query_count:].reshape(LANES, LANES).astype(jnp.int32)
        wrapped = index & (LANES - 1)
        low = jnp.take_along_axis(mine[rows, :LANES], wrapped, axis=1, mode="promise_in_bounds")
        high = jnp.take_along_axis(mine[rows, LANES:], wrapped, axis=1, mode="promise_in_bounds")
        value = raw[:, :query_count].reshape(LANES, LANES) * (1.0 / math.sqrt(32.0)) + jnp.where(
            index >= LANES, high, low
        )
        exponent = jnp.exp(value - jnp.max(value, axis=1, keepdims=True))
        weights[rows, :] = (exponent * (1.0 / jnp.sum(exponent, axis=1, keepdims=True))).astype(BF16)
        return carry

    lax.fori_loop(0, blocks, soften, 0, unroll=UB)

    def attend(b, carry):
        out = jnp.zeros((query_count, LANES), F32)
        for j in range(4):
            rows = pl.ds(pl.multiple_of(b * LANES + query_count * j, 32), query_count)
            gated = gate[rows, :] * dot(weights[rows, :], window_keys[4 * b + j])
            turned = gated if j == 2 else pltpu.roll(gated, (32 * j + 64) % LANES, 1)
            out = jnp.where(lane32 == j, turned, out)
        packed[p, pl.ds(pl.multiple_of(b * query_count, 32), query_count), :] = out.astype(BF16)
        for d in (2, 1, 3):
            gate_copy(b, d).start()
        return carry

    lax.fori_loop(0, blocks, attend, 0, unroll=UC)

    def wait_gate(b, carry):
        for d in range(1, n_pair):
            gate_arrive(b, d).wait_recv()
        return carry

    lax.fori_loop(0, blocks, wait_gate, 0)

    update = dot(packed[0], ow_cat[0:LANES, :])
    for h in range(1, n_pair):
        update = update + dot(packed[h], ow_cat[h * LANES : (h + 1) * LANES, :])
    for b in range(blocks):
        for j in range(4):
            at = b * LANES + 32 * j
            value = cond[first + at : first + at + 32, :].astype(F32) + update[
                32 * b : 32 * b + 32, j * LANES : (j + 1) * LANES
            ]
            atoms_bf[at : at + 32, :] = value.astype(BF16)
    atom_out[...] = atoms_bf[...]
    total = None
    for b in range(blocks):
        per_atom = jnp.maximum(dot(atoms_bf[b * LANES : (b + 1) * LANES, :], token_w[...]), 0.0).astype(BF16)
        term = dot(onehot_t[b], per_atom)
        total = term if total is None else total + term
    for s in range(GROUP):
        sums[s] = total[s * tok_dev : (s + 1) * tok_dev]
        sums_out[s] = total[s * tok_dev : (s + 1) * tok_dev].astype(BF16)
    for d in range(1, GROUP):
        sum_copy(d).start()
    eye = lax.broadcasted_iota(jnp.int32, (tok_dev, tok_dev), 0) == lax.broadcasted_iota(
        jnp.int32, (tok_dev, tok_dev), 1
    )
    count = jnp.sum(jnp.where(eye, counts[...].astype(F32), 0.0), axis=1, keepdims=True)
    result = sums[r]
    for d in range(1, GROUP):
        sum_copy(d).wait_recv()
        result = result + sums_in[d].astype(F32)
    token_out[...] = (result / count).astype(BF16)

    for d in range(1, GROUP):
        tp_copy(d).wait_send()
        sum_copy(d).wait_send()
    for d in range(1, n_pair):
        ow_copy(d).wait_send()
    to_right().wait_send()
    to_left().wait_send()

    def drain_bias(c, carry):
        for d in range(1, GROUP):
            bias_copy(c, d).wait_send()
        return carry

    lax.fori_loop(0, CHUNKS, drain_bias, 0)

    def drain_gate(b, carry):
        for d in range(1, n_pair):
            gate_copy(b, d).wait_send()
        return carry

    lax.fori_loop(0, blocks, drain_gate, 0)


def shards(
    trunk_single, atom_feature, pair_band, atom_token, token_counts, key_offsets,
    single_weight, attn_weight, bias_weight, out_weight, token_weight,
):
    n_dev = lax.axis_size("atoms")
    n_pair = lax.axis_size("pair")
    tok_dev, width = trunk_single.shape
    atom_dev = atom_feature.shape[0]
    blocks = atom_dev // LANES
    total_atoms = atom_token.shape[0]
    group_tok = GROUP * tok_dev
    ext = atom_dev + 2 * LANES
    vmem = pl.BlockSpec(memory_space=pltpu.VMEM)
    dma = pltpu.SemaphoreType.DMA
    return pl.pallas_call(
        functools.partial(kernel, (n_dev, n_pair, total_atoms)),
        out_shape=(
            jax.ShapeDtypeStruct((atom_dev, LANES), BF16),
            jax.ShapeDtypeStruct((tok_dev, width), BF16),
        ),
        in_specs=[
            pl.BlockSpec(memory_space=pl.ANY),
        ]
        * 11,
        out_specs=(vmem, vmem),
        scratch_shapes=[
            pltpu.VMEM(trunk_single.shape, BF16),
            pltpu.VMEM(atom_feature.shape, BF16),
            pltpu.VMEM((total_atoms // LANES, LANES), jnp.int32),
            pltpu.VMEM((1, tok_dev), jnp.int32),
            pltpu.SMEM(key_offsets.shape, jnp.int32),
            pltpu.VMEM(single_weight.shape, BF16),
            pltpu.VMEM((LANES, LANES), BF16),
            pltpu.VMEM((1, LANES), F32),
            pltpu.VMEM(token_weight.shape, BF16),
            dma((10,)),
            pltpu.VMEM(pair_band.shape, BF16),
            pltpu.VMEM((GROUP, tok_dev, LANES), BF16),
            pltpu.VMEM((GROUP, tok_dev, 2 * LANES), F32),
            pltpu.VMEM((ext, LANES), BF16),
            pltpu.VMEM((ext, LANES), F32),
            pltpu.VMEM((atom_dev // 32, 64, LANES), BF16),
            pltpu.VMEM((atom_dev, LANES), F32),
            pltpu.VMEM((atom_dev, group_tok), BF16),
            pltpu.VMEM((blocks, group_tok, LANES), BF16),
            pltpu.VMEM((blocks + 2, LANES, LANES), jnp.int32),
            pltpu.VMEM((blocks + 2, LANES), jnp.int32),
            pltpu.VMEM((atom_dev, 2 * LANES), F32),
            pltpu.VMEM((atom_dev // 32, 64, LANES), F32),
            pltpu.VMEM((atom_dev, LANES), BF16),
            pltpu.VMEM((atom_dev // 32, LANES, LANES), BF16),
            pltpu.VMEM((n_pair, 32, LANES), BF16),
            pltpu.VMEM((n_pair * LANES, 4 * LANES), BF16),
            pltpu.VMEM((GROUP, tok_dev, 2 * LANES), BF16),
            pltpu.VMEM((GROUP, tok_dev, 2 * LANES), BF16),
            pltpu.VMEM((n_pair, atom_dev // 4, LANES), BF16),
            pltpu.VMEM((atom_dev, LANES), BF16),
            pltpu.VMEM((GROUP, tok_dev, width), F32),
            pltpu.VMEM((GROUP, tok_dev, width), BF16),
            pltpu.VMEM((GROUP, tok_dev, width), BF16),
            dma((CHUNKS,)),
            dma((GROUP,)), dma((GROUP,)),
            dma((n_pair,)), dma((n_pair,)),
            dma((CHUNKS, GROUP)), dma((CHUNKS, GROUP)),
            dma((2,)), dma((2,)),
            dma((blocks, n_pair)), dma((blocks, n_pair)),
            dma((GROUP,)), dma((GROUP,)),
        ],
        compiler_params=pltpu.CompilerParams(
            collective_id=0, has_side_effects=True, vmem_limit_bytes=48 * 1024 * 1024
        ),
        name="encoder",
    )(
        *(
            pltpu.with_memory_space_constraint(value, pltpu.HBM)
            for value in (
                trunk_single,
                atom_feature,
                pair_band,
                atom_token.reshape(total_atoms // LANES, LANES),
                token_counts.reshape(1, tok_dev),
                key_offsets,
                single_weight,
                attn_weight.reshape(attn_weight.shape[0], attn_weight.shape[2]),
                bias_weight.reshape(1, bias_weight.shape[0]),
                out_weight,
                token_weight,
            )
        )
    )


def solution(mesh):
    placed = (
        P("atoms", None),
        P("atoms", None),
        P("atoms", None, None),
        P(),
        P("atoms"),
        P("atoms"),
        P(),
        P(None, "pair", None),
        P(None, "pair"),
        P("pair", None),
        P(),
    )
    return jax.shard_map(
        shards,
        mesh=mesh,
        in_specs=placed,
        out_specs=(P("atoms", None), P("atoms", None)),
        check_vma=False,
    )
```

```python
import functools
import math

import jax
import jax.numpy as jnp
from jax import lax
from jax.experimental import pallas as pl
from jax.experimental.pallas import tpu as pltpu
from jax.sharding import PartitionSpec as P

GROUP = 4
LANES = 128
MESH = pl.DeviceIdType.MESH
F32 = jnp.float32
BF16 = jnp.bfloat16
CHUNKS = 4
SEND = 3
PARTS = ((0, 6),)
NT = (((1,), (1,)), ((), ()))


def dot(a, b):
    return jnp.dot(a, b, preferred_element_type=F32)


def norm_rows(x):
    centred = x - jnp.mean(x, axis=-1, keepdims=True)
    spread = jnp.mean(centred * centred, axis=-1, keepdims=True)
    return centred * lax.rsqrt(spread + 1e-05)


def kernel(
    sizes,
    trunk_h, feat_h, band, tok_h, counts_h, koff_h, single_h, attn_h, bias_h, out_h, token_h,
    atom_out, token_out,
    trunk, feat, tok, counts, koff, single_w, attn_w, bias_w, token_w, in_sem,
    band_v, tp_all, bias_all, cond, keys, queries, gate, onehot, onehot_t, tok_info, tokl, mine,
    scores, weights, window_keys,
    ow_all, ow_cat, bias_hi, bias_lo, packed, atoms_bf, sums, sums_out, sums_in,
    band_sem, tp_send, tp_recv, ow_send, ow_recv, bias_send, bias_recv,
    halo_send, halo_recv, gate_send, gate_recv, sum_send, sum_recv,
):
    n_dev, n_pair, total_atoms = sizes
    tok_dev = trunk.shape[0]
    atom_dev = feat_h.shape[0]
    blocks = atom_dev // LANES
    reach = 96
    query_count = 32
    group_tok = GROUP * tok_dev
    part = tok_dev // CHUNKS
    a = lax.axis_index("atoms")
    p = lax.axis_index("pair")
    r = lax.rem(a, GROUP)
    base = a - r
    left = lax.rem(a + n_dev - 1, n_dev)
    right = lax.rem(a + 1, n_dev)

    def group_peer(d):
        return (base + lax.rem(r + d, GROUP), p)

    def pair_peer(d):
        return (a, lax.rem(p + d, n_pair))

    barrier = pltpu.get_barrier_semaphore()
    for d in range(1, GROUP):
        pl.semaphore_signal(barrier, inc=1, device_id=group_peer(d), device_id_type=MESH)
    for d in range(1, n_pair):
        pl.semaphore_signal(barrier, inc=1, device_id=pair_peer(d), device_id_type=MESH)
    pl.semaphore_signal(barrier, inc=1, device_id=(left, p), device_id_type=MESH)
    pl.semaphore_signal(barrier, inc=1, device_id=(right, p), device_id_type=MESH)

    def band_copy(c):
        rows = pl.ds(c * part, part)
        return pltpu.make_async_copy(band.at[rows], band_v.at[rows], band_sem.at[c])

    loads = [
        pltpu.make_async_copy(src, dst, in_sem.at[i])
        for i, (src, dst) in enumerate(
            (
                (trunk_h, trunk), (single_h, single_w), (out_h, ow_all.at[p]), (bias_h, bias_w), (tok_h, tok),
                (feat_h, feat.at[pl.ds(LANES, atom_dev)]), (attn_h, attn_w), (koff_h, koff), (token_h, token_w), (counts_h, counts),
            )
        )
    ]
    for load in loads[:4]:
        load.start()
    band_copy(0).start()
    for load in loads[4:]:
        load.start()
    for c in range(1, CHUNKS):
        band_copy(c).start()

    def remote(src, dst, send, recv, device):
        return pltpu.make_async_remote_copy(
            src_ref=src, dst_ref=dst, send_sem=send, recv_sem=recv, device_id=device, device_id_type=MESH
        )

    def sends(d, act):
        if d == 2:
            act()
        else:
            pl.when(r != (GROUP - 1 if d == 1 else 0))(act)

    def receives(d, act):
        if d == 2:
            act()
        else:
            pl.when(r != (0 if d == 1 else GROUP - 1))(act)

    def tp_rows(s):
        return tp_all.at[pl.ds(pl.multiple_of(s * tok_dev, 16), tok_dev)]

    def tp_copy(d):
        return remote(tp_rows(r), tp_rows(r), tp_send.at[d], tp_recv.at[d], group_peer(d))

    def tp_arrive(d):
        s = lax.rem(r + GROUP - d, GROUP)
        return remote(tp_rows(s), tp_rows(s), tp_send.at[d], tp_recv.at[d], group_peer(d))

    def tp_outside(neighbour):
        return remote(tp_rows(r), tp_rows(GROUP), tp_send.at[0], tp_recv.at[0], (neighbour, p))

    def outside(act):
        pl.when(r == 0)(lambda: act(tp_outside(left)))
        pl.when(r == GROUP - 1)(lambda: act(tp_outside(right)))

    def ow_copy(d):
        return remote(ow_all.at[p], ow_all.at[p], ow_send.at[d], ow_recv.at[d], pair_peer(d))

    def ow_arrive(d):
        s = lax.rem(p + n_pair - d, n_pair)
        return remote(ow_all.at[s], ow_all.at[s], ow_send.at[d], ow_recv.at[d], pair_peer(d))

    def bias_copy(c, d):
        rows = pl.ds(c * part, part)
        return remote(
            bias_all.at[r, rows], bias_all.at[r, rows], bias_send.at[c, d], bias_recv.at[c, d], group_peer(d)
        )

    def bias_arrive(c, d):
        s = lax.rem(r + GROUP - d, GROUP)
        rows = pl.ds(c * part, part)
        return remote(
            bias_all.at[s, rows], bias_all.at[s, rows], bias_send.at[c, d], bias_recv.at[c, d], group_peer(d)
        )

    first, last = LANES, LANES + atom_dev

    def to_right():
        return remote(
            feat_h.at[pl.ds(atom_dev - reach, reach)], feat.at[pl.ds(first - reach, reach)],
            halo_send.at[0], halo_recv.at[0], (right, p),
        )

    def to_left():
        return remote(
            feat_h.at[pl.ds(0, reach)], feat.at[pl.ds(last, reach)],
            halo_send.at[1], halo_recv.at[1], (left, p),
        )

    def gate_copy(b, d):
        rows = pl.ds(b * query_count * SEND, query_count * SEND)
        return remote(
            packed.at[p, rows], packed.at[p, rows], gate_send.at[b, d], gate_recv.at[b, d], pair_peer(d)
        )

    def gate_arrive(b, d):
        s = lax.rem(p + n_pair - d, n_pair)
        rows = pl.ds(b * query_count * SEND, query_count * SEND)
        return remote(
            packed.at[s, rows], packed.at[s, rows], gate_send.at[b, d], gate_recv.at[b, d], pair_peer(d)
        )

    def sum_copy(c, d):
        t = lax.rem(r + d, GROUP)
        return remote(sums_out.at[t, c], sums_in.at[d, c], sum_send.at[c, d], sum_recv.at[c, d], group_peer(d))

    for load in loads[:3]:
        load.wait()
    tp_all[pl.ds(pl.multiple_of(r * tok_dev, 16), tok_dev), :] = dot(norm_rows(trunk[...].astype(F32)).astype(BF16), single_w[...]).astype(BF16)
    loads[3].wait()
    w = bias_w[...]
    w_hi = w.astype(BF16).astype(F32)
    w_mid = (w - w_hi).astype(BF16).astype(F32)
    w_lo = w - w_hi - w_mid
    w_total = jnp.sum(w, axis=1, keepdims=True)
    row_id = lax.broadcasted_iota(jnp.int32, (16, LANES), 0)
    parts = jnp.where(
        row_id == 0, w_hi, jnp.where(row_id == 1, w_mid, jnp.where(row_id == 2, w_lo, jnp.where(row_id == 3, 1.0, 0.0)))
    ).astype(BF16)
    lane8 = lax.broadcasted_iota(jnp.int32, (8, LANES), 1)
    diag_mask = lax.rem(lane8, 8) == lax.broadcasted_iota(jnp.int32, (8, LANES), 0)
    lane_group = lane8 // 8

    def band_rows(x):
        g = lax.dot_general(jnp.concatenate([x, parts], axis=0), x, NT, preferred_element_type=F32)
        acc = g[0:8]
        for s in range(1, LANES // 8):
            acc = jnp.where(lane_group == s, g[8 * s : 8 * s + 8], acc)
        squares = jnp.sum(jnp.where(diag_mask, acc, 0.0), axis=0, keepdims=True)
        products = g[LANES : LANES + 1] + g[LANES + 1 : LANES + 2] + g[LANES + 2 : LANES + 3]
        return products, g[LANES + 3 : LANES + 4], squares

    def band_step(start):
        halves = []
        for half in range(2):
            got = [band_rows(band_v[start + t, half * LANES : (half + 1) * LANES, :]) for t in range(8)]
            products, total, squares = (jnp.concatenate(list(v), axis=0) for v in zip(*got))
            mean = total * (1.0 / LANES)
            spread = jnp.maximum(squares * (1.0 / LANES) - mean * mean, 0.0)
            halves.append((products - mean * w_total) * lax.rsqrt(spread + 1e-05))
        bias_all[r, pl.ds(pl.multiple_of(start, 8), 8), :] = jnp.concatenate(halves, axis=1)

    def band_chunk(c):
        band_copy(c).wait()
        for i in range(part // 8):
            band_step(c * part + i * 8)

    def send_bias(c):
        for d in (2, 1, 3):
            sends(d, lambda: bias_copy(c, d).start())

    def clear(slot, distance):
        bias_all[slot] = jnp.zeros(bias_all.shape[1:], F32)
        sums_in[distance] = jnp.zeros(sums_in.shape[1:], BF16)

    pl.when(r == 0)(lambda: clear(GROUP - 1, 1))
    pl.when(r == GROUP - 1)(lambda: clear(0, GROUP - 1))

    feat[0 : first - reach, :] = jnp.zeros((first - reach, LANES), BF16)
    feat[last + reach : last + LANES, :] = jnp.zeros((LANES - reach, LANES), BF16)
    tp_all[(GROUP + 1) * tok_dev :, :] = jnp.zeros((tp_all.shape[0] - (GROUP + 1) * tok_dev, LANES), BF16)

    @pl.when((r > 0) & (r < GROUP - 1))
    def no_outside():
        tp_all[GROUP * tok_dev : (GROUP + 1) * tok_dev, :] = jnp.zeros((tok_dev, LANES), BF16)

    band_chunk(0)
    pl.semaphore_wait(barrier, 3 + n_pair - 1 + 2)
    for d in (2, 1, 3):
        tp_copy(d).start()
    outside(lambda copy: copy.start())
    to_right().start()
    to_left().start()
    send_bias(0)
    for d in range(1, n_pair):
        ow_copy(d).start()
    for c in range(1, CHUNKS):
        band_chunk(c)
        send_bias(c)

    token_base = (base * tok_dev).astype(jnp.int32)
    for load in loads[4:]:
        load.wait()
    for i in range(blocks + 2):
        row = lax.rem(a * blocks + i - 1 + total_atoms // LANES, total_atoms // LANES)
        tokl[i : i + 1, :] = tok[pl.ds(row, 1), :]
    lane1 = lax.broadcasted_iota(jnp.int32, (LANES, LANES), 1)
    sub = lax.broadcasted_iota(jnp.int32, (group_tok, LANES), 0)
    for i in range(blocks + 2):
        tok_row = tokl[i : i + 1, :] - token_base
        tok_col = jnp.broadcast_to(tok_row, (LANES, LANES)).astype(F32).T.astype(jnp.int32)
        tok_info[i] = tok_col
        wanted = jnp.where(tok_col < 0, tok_col + (GROUP + 1) * tok_dev, tok_col)
        onehot[i * LANES : (i + 1) * LANES, :] = jnp.concatenate(
            [(wanted == lane1 + k * LANES).astype(F32).astype(BF16) for k in range(onehot.shape[1] // LANES)], axis=1
        )
        if 1 <= i <= blocks:
            onehot_t[:, (i - 1) * LANES : i * LANES] = (
                (jnp.broadcast_to(tok_row, (group_tok, LANES)) == sub).astype(F32).astype(BF16)
            )

    for d in range(1, GROUP):
        tp_arrive(d).wait_recv()
    outside(lambda copy: copy.wait_recv())
    to_right().wait_recv()
    to_left().wait_recv()
    for i in range(blocks + 2):
        rows = slice(i * LANES, (i + 1) * LANES)
        chosen = dot(onehot[rows, :], tp_all[...]).astype(BF16)
        cond[rows, :] = (feat[rows, :].astype(F32) + chosen.astype(F32)).astype(BF16)

    aw = attn_w[...]
    aw32 = aw.astype(F32)
    head = lane1 // 32
    q_w = jnp.where(head == 1, pltpu.roll(aw32, 32, 1), 0.0).astype(BF16)
    g_w = jnp.where(head == 2, pltpu.roll(aw32, LANES - 32, 1), 0.0).astype(BF16)
    kv_lane = (head == 1) | (head == 2)

    def key_rows(i, normed):
        place = lax.broadcasted_iota(jnp.int32, (LANES, LANES), 0) + (a * atom_dev + (i - 1) * LANES)
        absent = jnp.where((place >= 0) & (place < total_atoms), 0.0, -1e30)
        token = tok_info[i] + LANES
        info = jnp.where(
            lane1 == 0,
            (token >> 4).astype(F32),
            jnp.where(lane1 == 1, (token & 15).astype(F32), jnp.where(lane1 == 3, absent, jnp.where((lane1 == 2) | (lane1 == 4), 1.0, 0.0))),
        )
        keys[pl.ds(pl.multiple_of(i * LANES, LANES), LANES), :] = jnp.where(
            kv_lane, dot(normed, aw).astype(BF16).astype(F32), info
        )

    def proj_block(b, carry):
        rows = pl.ds(pl.multiple_of(b * LANES, LANES), LANES)
        normed = norm_rows(cond[pl.ds(pl.multiple_of(first + b * LANES, LANES), LANES), :].astype(F32)).astype(BF16)
        key_rows(b + 1, normed)
        query = jnp.where(lane1 == 3, 1.0, dot(normed, q_w)).astype(BF16)
        token = tok_info[b + 1] + LANES
        against = jnp.where(
            lane1 == 0,
            16.0,
            jnp.where(
                lane1 == 1,
                1.0,
                jnp.where(
                    lane1 == 2,
                    (LANES - (token >> 4) * 16).astype(F32),
                    jnp.where(lane1 == 4, (-(token & 15)).astype(F32), 0.0),
                ),
            ),
        ).astype(BF16)
        for j in range(4):
            queries[4 * b + j, 0:32, :] = query[32 * j : 32 * j + 32]
            queries[4 * b + j, 32:64, :] = against[32 * j : 32 * j + 32]
        gate[rows, :] = jax.nn.sigmoid(dot(normed, g_w).astype(BF16).astype(F32))
        return carry

    lax.fori_loop(0, blocks, proj_block, 0, unroll=True)
    for i in (0, blocks + 1):
        key_rows(i, norm_rows(cond[i * LANES : (i + 1) * LANES, :].astype(F32)).astype(BF16))

    for d in range(1, n_pair):
        ow_arrive(d).wait_recv()
    ow_cat[...] = jnp.zeros(ow_cat.shape, BF16)
    for h in range(n_pair):
        for j in range(4):
            ow_cat[h * LANES + 32 * j : h * LANES + 32 * j + 32, j * LANES : (j + 1) * LANES] = ow_all[h]

    lane32 = lax.broadcasted_iota(jnp.int32, (query_count, LANES), 1) // 32
    windows = atom_dev // query_count

    def score(w, carry):
        start = LANES + query_count * w + koff[w]
        window = keys[pl.ds(start, LANES), :].astype(BF16)
        window_keys[w] = window
        scores[w] = lax.dot_general(queries[w], window, NT, preferred_element_type=F32)
        return carry


    for w in range(windows):
        score(w, 0)

    for c in range(CHUNKS):
        for d in range(1, GROUP):
            receives(d, lambda: bias_arrive(c, d).wait_recv())
    for s in range(GROUP):
        whole = bias_all[s]
        high = whole.astype(BF16)
        bias_hi[s] = high
        bias_lo[s] = (whole - high.astype(F32)).astype(BF16)

    both = jnp.concatenate([bias_hi[...].reshape(group_tok, 2 * LANES), bias_lo[...].reshape(group_tok, 2 * LANES)], axis=0)
    for b in range(blocks):
        pick = onehot[first + b * LANES : first + (b + 1) * LANES, :group_tok]
        mine[b * LANES : (b + 1) * LANES, :] = dot(jnp.concatenate([pick, pick], axis=1), both)

    def soften(b, carry):
        rows = pl.ds(pl.multiple_of(b * LANES, LANES), LANES)
        raw = scores[pl.ds(4 * b, 4)]
        index = raw[:, query_count:].reshape(LANES, LANES).astype(jnp.int32)
        wrapped = index & (LANES - 1)
        low = jnp.take_along_axis(mine[rows, :LANES], wrapped, axis=1, mode="promise_in_bounds")
        high = jnp.take_along_axis(mine[rows, LANES:], wrapped, axis=1, mode="promise_in_bounds")
        value = raw[:, :query_count].reshape(LANES, LANES) * (1.0 / math.sqrt(32.0)) + jnp.where(
            index >= LANES, high, low
        )
        exponent = jnp.exp(value - jnp.max(value, axis=1, keepdims=True))
        weights[rows, :] = (exponent * (1.0 / jnp.sum(exponent, axis=1, keepdims=True))).astype(BF16)
        return carry


    def attend(b, carry):
        out = jnp.zeros((query_count, LANES), F32)
        for j in range(4):
            rows = pl.ds(pl.multiple_of(b * LANES + query_count * j, 32), query_count)
            gated = gate[rows, :] * dot(weights[rows, :], window_keys[4 * b + j])
            turned = gated if j == 2 else pltpu.roll(gated, (32 * j + 64) % LANES, 1)
            out = jnp.where(lane32 == j, turned, out)
        packed[p, pl.ds(pl.multiple_of(b * query_count, 32), query_count), :] = out.astype(BF16)
        return carry

    for b in range(blocks):
        soften(b, 0)
    for b in range(blocks):
        attend(b, 0)

    for b in range(blocks // SEND):
        for d in (2, 1, 3):
            gate_copy(b, d).start()

    column_blocks = sums.shape[1]
    for k, (begin, end) in enumerate(PARTS):
        for b in range(blocks // SEND):
            for d in range(1, n_pair):
                gate_arrive(b, d).wait_recv()
        rows = slice(32 * begin, 32 * end)
        update = dot(packed[0, rows], ow_cat[0:LANES, :])
        for h in range(1, n_pair):
            update = update + dot(packed[h, rows], ow_cat[h * LANES : (h + 1) * LANES, :])
        for b in range(begin, end):
            for j in range(4):
                at = b * LANES + 32 * j
                value = cond[first + at : first + at + 32, :].astype(F32) + update[
                    32 * (b - begin) : 32 * (b - begin) + 32, j * LANES : (j + 1) * LANES
                ]
                atoms_bf[at : at + 32, :] = value.astype(BF16)
        span = slice(begin * LANES, end * LANES)
        atom_out[span, :] = atoms_bf[span, :]
        for c in range(column_blocks):
            per_atom = jnp.maximum(dot(atoms_bf[span, :], token_w[:, c * LANES : (c + 1) * LANES]), 0.0).astype(BF16)
            total = dot(onehot_t[:, span], per_atom)
            for t in range(GROUP):
                here = total[t * tok_dev : (t + 1) * tok_dev]
                if k > 0:
                    here = here + sums[t, c]
                sums[t, c] = here
                if k == len(PARTS) - 1:
                    sums_out[t, c] = here.astype(BF16)
            if k == len(PARTS) - 1:
                for d in (2, 1, 3):
                    sends(d, lambda: sum_copy(c, d).start())
    eye = lax.broadcasted_iota(jnp.int32, (tok_dev, tok_dev), 0) == lax.broadcasted_iota(
        jnp.int32, (tok_dev, tok_dev), 1
    )
    count = jnp.sum(jnp.where(eye, counts[...].astype(F32), 0.0), axis=1, keepdims=True)
    inverse = 1.0 / count
    for c in range(column_blocks):
        for d in range(1, GROUP):
            receives(d, lambda: sum_copy(c, d).wait_recv())
        result = sums[r, c]
        for d in range(1, GROUP):
            result = result + sums_in[d, c].astype(F32)
        token_out[:, c * LANES : (c + 1) * LANES] = (result * inverse).astype(BF16)

    for d in range(1, GROUP):
        tp_copy(d).wait_send()
        for c in range(column_blocks):
            sends(d, lambda: sum_copy(c, d).wait_send())
        for c in range(CHUNKS):
            sends(d, lambda: bias_copy(c, d).wait_send())
    for d in range(1, n_pair):
        ow_copy(d).wait_send()
        for b in range(blocks // SEND):
            gate_copy(b, d).wait_send()
    outside(lambda copy: copy.wait_send())
    to_right().wait_send()
    to_left().wait_send()


def shards(
    trunk_single, atom_feature, pair_band, atom_token, token_counts, key_offsets,
    single_weight, attn_weight, bias_weight, out_weight, token_weight,
):
    n_dev = lax.axis_size("atoms")
    n_pair = lax.axis_size("pair")
    tok_dev, width = trunk_single.shape
    atom_dev = atom_feature.shape[0]
    blocks = atom_dev // LANES
    total_atoms = atom_token.shape[0]
    group_tok = GROUP * tok_dev
    ext = atom_dev + 2 * LANES
    vmem = pl.BlockSpec(memory_space=pltpu.VMEM)
    dma = pltpu.SemaphoreType.DMA
    return pl.pallas_call(
        functools.partial(kernel, (n_dev, n_pair, total_atoms)),
        out_shape=(
            jax.ShapeDtypeStruct((atom_dev, LANES), BF16),
            jax.ShapeDtypeStruct((tok_dev, width), BF16),
        ),
        in_specs=[
            pl.BlockSpec(memory_space=pl.ANY),
        ]
        * 11,
        out_specs=(vmem, vmem),
        scratch_shapes=[
            pltpu.VMEM(trunk_single.shape, BF16),
            pltpu.VMEM((ext, LANES), BF16),
            pltpu.VMEM((total_atoms // LANES, LANES), jnp.int32),
            pltpu.VMEM((1, tok_dev), jnp.int32),
            pltpu.SMEM(key_offsets.shape, jnp.int32),
            pltpu.VMEM(single_weight.shape, BF16),
            pltpu.VMEM((LANES, LANES), BF16),
            pltpu.VMEM((1, LANES), F32),
            pltpu.VMEM(token_weight.shape, BF16),
            dma((10,)),
            pltpu.VMEM(pair_band.shape, BF16),
            pltpu.VMEM((group_tok + LANES, LANES), BF16),
            pltpu.VMEM((GROUP, tok_dev, 2 * LANES), F32),
            pltpu.VMEM((ext, LANES), BF16),
            pltpu.VMEM((ext, LANES), F32),
            pltpu.VMEM((atom_dev // 32, 64, LANES), BF16),
            pltpu.VMEM((atom_dev, LANES), F32),
            pltpu.VMEM((ext, group_tok + LANES), BF16),
            pltpu.VMEM((group_tok, atom_dev), BF16),
            pltpu.VMEM((blocks + 2, LANES, LANES), jnp.int32),
            pltpu.VMEM((blocks + 2, LANES), jnp.int32),
            pltpu.VMEM((atom_dev, 2 * LANES), F32),
            pltpu.VMEM((atom_dev // 32, 64, LANES), F32),
            pltpu.VMEM((atom_dev, LANES), BF16),
            pltpu.VMEM((atom_dev // 32, LANES, LANES), BF16),
            pltpu.VMEM((n_pair, 32, LANES), BF16),
            pltpu.VMEM((n_pair * LANES, 4 * LANES), BF16),
            pltpu.VMEM((GROUP, tok_dev, 2 * LANES), BF16),
            pltpu.VMEM((GROUP, tok_dev, 2 * LANES), BF16),
            pltpu.VMEM((n_pair, atom_dev // 4, LANES), BF16),
            pltpu.VMEM((atom_dev, LANES), BF16),
            pltpu.VMEM((GROUP, width // LANES, tok_dev, LANES), F32),
            pltpu.VMEM((GROUP, width // LANES, tok_dev, LANES), BF16),
            pltpu.VMEM((GROUP, width // LANES, tok_dev, LANES), BF16),
            dma((CHUNKS,)),
            dma((GROUP,)), dma((GROUP,)),
            dma((n_pair,)), dma((n_pair,)),
            dma((CHUNKS, GROUP)), dma((CHUNKS, GROUP)),
            dma((2,)), dma((2,)),
            dma((blocks, n_pair)), dma((blocks, n_pair)),
            dma((width // LANES, GROUP)), dma((width // LANES, GROUP)),
        ],
        compiler_params=pltpu.CompilerParams(
            collective_id=0, has_side_effects=True, vmem_limit_bytes=48 * 1024 * 1024
        ),
        name="encoder",
    )(
        *(
            pltpu.with_memory_space_constraint(value, pltpu.HBM)
            for value in (
                trunk_single,
                atom_feature,
                pair_band,
                atom_token.reshape(total_atoms // LANES, LANES),
                token_counts.reshape(1, tok_dev),
                key_offsets,
                single_weight,
                attn_weight.reshape(attn_weight.shape[0], attn_weight.shape[2]),
                bias_weight.reshape(1, bias_weight.shape[0]),
                out_weight,
                token_weight,
            )
        )
    )


def solution(mesh):
    placed = (
        P("atoms", None),
        P("atoms", None),
        P("atoms", None, None),
        P(),
        P("atoms"),
        P("atoms"),
        P(),
        P(None, "pair", None),
        P(None, "pair"),
        P("pair", None),
        P(),
    )
    return jax.shard_map(
        shards,
        mesh=mesh,
        in_specs=placed,
        out_specs=(P("atoms", None), P("atoms", None)),
        check_vma=False,
    )
```

```python
import functools
import math

import jax
import jax.numpy as jnp
from jax import lax
from jax.experimental import pallas as pl
from jax.experimental.pallas import tpu as pltpu
from jax.sharding import PartitionSpec as P

GROUP = 4
LANES = 128
MESH = pl.DeviceIdType.MESH
F32 = jnp.float32
BF16 = jnp.bfloat16
CHUNKS = 4
SEND = 6
PARTS = ((0, 6),)
NT = (((1,), (1,)), ((), ()))


def dot(a, b):
    return jnp.dot(a, b, preferred_element_type=F32)


def norm_rows(x):
    centred = x - jnp.mean(x, axis=-1, keepdims=True)
    spread = jnp.mean(centred * centred, axis=-1, keepdims=True)
    return centred * lax.rsqrt(spread + 1e-05)


def kernel(
    sizes,
    trunk_h, feat_h, band, tok_h, counts_h, koff_h, single_h, attn_h, bias_h, out_h, token_h,
    atom_out, token_out,
    trunk, feat, tok, counts, koff, single_w, attn_w, bias_w, token_w, in_sem,
    band_v, tp_all, bias_all, cond, keys, queries, gate, onehot, onehot_t, tok_info, tokl, mine,
    scores, weights, window_keys,
    ow_all, ow_cat, bias_hi, bias_lo, packed, atoms_bf, sums, sums_out, sums_in,
    band_sem, tp_send, tp_recv, ow_send, ow_recv, bias_send, bias_recv,
    halo_send, halo_recv, gate_send, gate_recv, sum_send, sum_recv,
):
    n_dev, n_pair, total_atoms = sizes
    tok_dev = trunk.shape[0]
    atom_dev = feat_h.shape[0]
    blocks = atom_dev // LANES
    reach = 96
    query_count = 32
    group_tok = GROUP * tok_dev
    part = tok_dev // CHUNKS
    a = lax.axis_index("atoms")
    p = lax.axis_index("pair")
    r = lax.rem(a, GROUP)
    base = a - r
    left = lax.rem(a + n_dev - 1, n_dev)
    right = lax.rem(a + 1, n_dev)

    def group_peer(d):
        return (base + lax.rem(r + d, GROUP), p)

    def pair_peer(d):
        return (a, lax.rem(p + d, n_pair))

    barrier = pltpu.get_barrier_semaphore()
    for d in range(1, GROUP):
        pl.semaphore_signal(barrier, inc=1, device_id=group_peer(d), device_id_type=MESH)
    for d in range(1, n_pair):
        pl.semaphore_signal(barrier, inc=1, device_id=pair_peer(d), device_id_type=MESH)
    pl.semaphore_signal(barrier, inc=1, device_id=(left, p), device_id_type=MESH)
    pl.semaphore_signal(barrier, inc=1, device_id=(right, p), device_id_type=MESH)

    def band_copy(c):
        rows = pl.ds(c * part, part)
        return pltpu.make_async_copy(band.at[rows], band_v.at[rows], band_sem.at[c])

    loads = [
        pltpu.make_async_copy(src, dst, in_sem.at[i])
        for i, (src, dst) in enumerate(
            (
                (trunk_h, trunk), (single_h, single_w), (out_h, ow_all.at[p]), (bias_h, bias_w), (tok_h, tok),
                (feat_h, feat.at[pl.ds(LANES, atom_dev)]), (attn_h, attn_w), (koff_h, koff), (token_h, token_w), (counts_h, counts),
            )
        )
    ]
    for load in loads[:4]:
        load.start()
    band_copy(0).start()
    for load in loads[4:]:
        load.start()
    for c in range(1, CHUNKS):
        band_copy(c).start()

    def remote(src, dst, send, recv, device):
        return pltpu.make_async_remote_copy(
            src_ref=src, dst_ref=dst, send_sem=send, recv_sem=recv, device_id=device, device_id_type=MESH
        )

    def sends(d, act):
        if d == 2:
            act()
        else:
            pl.when(r != (GROUP - 1 if d == 1 else 0))(act)

    def receives(d, act):
        if d == 2:
            act()
        else:
            pl.when(r != (0 if d == 1 else GROUP - 1))(act)

    def tp_rows(s):
        return tp_all.at[pl.ds(pl.multiple_of(s * tok_dev, 16), tok_dev)]

    def tp_copy(d):
        return remote(tp_rows(r), tp_rows(r), tp_send.at[d], tp_recv.at[d], group_peer(d))

    def tp_arrive(d):
        s = lax.rem(r + GROUP - d, GROUP)
        return remote(tp_rows(s), tp_rows(s), tp_send.at[d], tp_recv.at[d], group_peer(d))

    def tp_outside(neighbour):
        return remote(tp_rows(r), tp_rows(GROUP), tp_send.at[0], tp_recv.at[0], (neighbour, p))

    def outside(act):
        pl.when(r == 0)(lambda: act(tp_outside(left)))
        pl.when(r == GROUP - 1)(lambda: act(tp_outside(right)))

    def ow_copy(d):
        return remote(ow_all.at[p], ow_all.at[p], ow_send.at[d], ow_recv.at[d], pair_peer(d))

    def ow_arrive(d):
        s = lax.rem(p + n_pair - d, n_pair)
        return remote(ow_all.at[s], ow_all.at[s], ow_send.at[d], ow_recv.at[d], pair_peer(d))

    def bias_copy(c, d):
        rows = pl.ds(c * part, part)
        return remote(
            bias_all.at[r, rows], bias_all.at[r, rows], bias_send.at[c, d], bias_recv.at[c, d], group_peer(d)
        )

    def bias_arrive(c, d):
        s = lax.rem(r + GROUP - d, GROUP)
        rows = pl.ds(c * part, part)
        return remote(
            bias_all.at[s, rows], bias_all.at[s, rows], bias_send.at[c, d], bias_recv.at[c, d], group_peer(d)
        )

    first, last = LANES, LANES + atom_dev

    def to_right():
        return remote(
            feat_h.at[pl.ds(atom_dev - reach, reach)], feat.at[pl.ds(first - reach, reach)],
            halo_send.at[0], halo_recv.at[0], (right, p),
        )

    def to_left():
        return remote(
            feat_h.at[pl.ds(0, reach)], feat.at[pl.ds(last, reach)],
            halo_send.at[1], halo_recv.at[1], (left, p),
        )

    def gate_copy(b, d):
        rows = pl.ds(b * query_count * SEND, query_count * SEND)
        return remote(
            packed.at[p, rows], packed.at[p, rows], gate_send.at[b, d], gate_recv.at[b, d], pair_peer(d)
        )

    def gate_arrive(b, d):
        s = lax.rem(p + n_pair - d, n_pair)
        rows = pl.ds(b * query_count * SEND, query_count * SEND)
        return remote(
            packed.at[s, rows], packed.at[s, rows], gate_send.at[b, d], gate_recv.at[b, d], pair_peer(d)
        )

    def sum_copy(c, d):
        t = lax.rem(r + d, GROUP)
        return remote(sums_out.at[t], sums_in.at[d], sum_send.at[c, d], sum_recv.at[c, d], group_peer(d))

    for load in loads[:3]:
        load.wait()
    pl.semaphore_wait(barrier, 3 + n_pair - 1 + 2)
    to_right().start()
    to_left().start()
    for d in range(1, n_pair):
        ow_copy(d).start()
    tp_all[pl.ds(pl.multiple_of(r * tok_dev, 16), tok_dev), :] = dot(norm_rows(trunk[...].astype(F32)).astype(BF16), single_w[...]).astype(BF16)
    loads[3].wait()
    w = bias_w[...]
    w_hi = w.astype(BF16).astype(F32)
    w_mid = (w - w_hi).astype(BF16).astype(F32)
    w_lo = w - w_hi - w_mid
    w_total = jnp.sum(w, axis=1, keepdims=True)
    row_id = lax.broadcasted_iota(jnp.int32, (16, LANES), 0)
    parts = jnp.where(
        row_id == 0, w_hi, jnp.where(row_id == 1, w_mid, jnp.where(row_id == 2, w_lo, jnp.where(row_id == 3, 1.0, 0.0)))
    ).astype(BF16)
    lane8 = lax.broadcasted_iota(jnp.int32, (8, LANES), 1)
    diag_mask = lax.rem(lane8, 8) == lax.broadcasted_iota(jnp.int32, (8, LANES), 0)
    lane_group = lane8 // 8

    def band_rows(x):
        g = lax.dot_general(jnp.concatenate([x, parts], axis=0), x, NT, preferred_element_type=F32)
        acc = g[0:8]
        for s in range(1, LANES // 8):
            acc = jnp.where(lane_group == s, g[8 * s : 8 * s + 8], acc)
        squares = jnp.sum(jnp.where(diag_mask, acc, 0.0), axis=0, keepdims=True)
        products = g[LANES : LANES + 1] + g[LANES + 1 : LANES + 2] + g[LANES + 2 : LANES + 3]
        return products, g[LANES + 3 : LANES + 4], squares

    def band_step(start):
        halves = []
        for half in range(2):
            got = [band_rows(band_v[start + t, half * LANES : (half + 1) * LANES, :]) for t in range(8)]
            products, total, squares = (jnp.concatenate(list(v), axis=0) for v in zip(*got))
            mean = total * (1.0 / LANES)
            spread = jnp.maximum(squares * (1.0 / LANES) - mean * mean, 0.0)
            halves.append((products - mean * w_total) * lax.rsqrt(spread + 1e-05))
        bias_all[r, pl.ds(pl.multiple_of(start, 8), 8), :] = jnp.concatenate(halves, axis=1)

    def band_chunk(c):
        band_copy(c).wait()
        for i in range(part // 8):
            band_step(c * part + i * 8)

    def send_bias(c):
        for d in (2, 1, 3):
            sends(d, lambda: bias_copy(c, d).start())

    def clear(slot, distance):
        bias_all[slot] = jnp.zeros(bias_all.shape[1:], F32)
        sums_in[distance] = jnp.zeros(sums_in.shape[1:], BF16)

    pl.when(r == 0)(lambda: clear(GROUP - 1, 1))
    pl.when(r == GROUP - 1)(lambda: clear(0, GROUP - 1))

    feat[0 : first - reach, :] = jnp.zeros((first - reach, LANES), BF16)
    feat[last + reach : last + LANES, :] = jnp.zeros((LANES - reach, LANES), BF16)
    tp_all[(GROUP + 1) * tok_dev :, :] = jnp.zeros((tp_all.shape[0] - (GROUP + 1) * tok_dev, LANES), BF16)

    @pl.when((r > 0) & (r < GROUP - 1))
    def no_outside():
        tp_all[GROUP * tok_dev : (GROUP + 1) * tok_dev, :] = jnp.zeros((tok_dev, LANES), BF16)

    for d in (2, 1, 3):
        tp_copy(d).start()
    outside(lambda copy: copy.start())
    for c in range(CHUNKS):
        band_chunk(c)
        send_bias(c)

    token_base = (base * tok_dev).astype(jnp.int32)
    for load in loads[4:]:
        load.wait()
    for i in range(blocks + 2):
        row = lax.rem(a * blocks + i - 1 + total_atoms // LANES, total_atoms // LANES)
        tokl[i : i + 1, :] = tok[pl.ds(row, 1), :]
    lane1 = lax.broadcasted_iota(jnp.int32, (LANES, LANES), 1)
    sub = lax.broadcasted_iota(jnp.int32, (group_tok, LANES), 0)
    for i in range(blocks + 2):
        tok_row = tokl[i : i + 1, :] - token_base
        tok_col = jnp.broadcast_to(tok_row, (LANES, LANES)).astype(F32).T.astype(jnp.int32)
        tok_info[i] = tok_col
        wanted = jnp.where(tok_col < 0, tok_col + (GROUP + 1) * tok_dev, tok_col)
        onehot[i * LANES : (i + 1) * LANES, :] = jnp.concatenate(
            [(wanted == lane1 + k * LANES).astype(F32).astype(BF16) for k in range(onehot.shape[1] // LANES)], axis=1
        )
        if 1 <= i <= blocks:
            onehot_t[:, (i - 1) * LANES : i * LANES] = (
                (jnp.broadcast_to(tok_row, (group_tok, LANES)) == sub).astype(F32).astype(BF16)
            )

    for d in range(1, GROUP):
        tp_arrive(d).wait_recv()
    outside(lambda copy: copy.wait_recv())
    to_right().wait_recv()
    to_left().wait_recv()
    for i in range(blocks + 2):
        rows = slice(i * LANES, (i + 1) * LANES)
        chosen = dot(onehot[rows, :], tp_all[...]).astype(BF16)
        cond[rows, :] = (feat[rows, :].astype(F32) + chosen.astype(F32)).astype(BF16)

    aw = attn_w[...]
    aw32 = aw.astype(F32)
    head = lane1 // 32
    q_w = jnp.where(head == 1, pltpu.roll(aw32, 32, 1), 0.0).astype(BF16)
    g_w = jnp.where(head == 2, pltpu.roll(aw32, LANES - 32, 1), 0.0).astype(BF16)
    kv_lane = (head == 1) | (head == 2)

    w_all = jnp.concatenate([aw, q_w, g_w], axis=1)

    def key_rows(i, product):
        place = lax.broadcasted_iota(jnp.int32, (LANES, LANES), 0) + (a * atom_dev + (i - 1) * LANES)
        absent = jnp.where((place >= 0) & (place < total_atoms), 0.0, -1e30)
        token = tok_info[i] + LANES
        info = jnp.where(
            lane1 == 0,
            (token >> 4).astype(F32),
            jnp.where(lane1 == 1, (token & 15).astype(F32), jnp.where(lane1 == 3, absent, jnp.where((lane1 == 2) | (lane1 == 4), 1.0, 0.0))),
        )
        keys[pl.ds(pl.multiple_of(i * LANES, LANES), LANES), :] = jnp.where(
            kv_lane, product.astype(BF16).astype(F32), info
        )

    def proj_block(b, carry):
        rows = pl.ds(pl.multiple_of(b * LANES, LANES), LANES)
        normed = norm_rows(cond[pl.ds(pl.multiple_of(first + b * LANES, LANES), LANES), :].astype(F32)).astype(BF16)
        product = dot(normed, w_all)
        key_rows(b + 1, product[:, :LANES])
        query = jnp.where(lane1 == 3, 1.0, product[:, LANES : 2 * LANES]).astype(BF16)
        token = tok_info[b + 1] + LANES
        against = jnp.where(
            lane1 == 0,
            16.0,
            jnp.where(
                lane1 == 1,
                1.0,
                jnp.where(
                    lane1 == 2,
                    (LANES - (token >> 4) * 16).astype(F32),
                    jnp.where(lane1 == 4, (-(token & 15)).astype(F32), 0.0),
                ),
            ),
        ).astype(BF16)
        for j in range(4):
            queries[4 * b + j, 0:32, :] = query[32 * j : 32 * j + 32]
            queries[4 * b + j, 32:64, :] = against[32 * j : 32 * j + 32]
        gate[rows, :] = jax.nn.sigmoid(product[:, 2 * LANES :].astype(BF16).astype(F32))
        return carry

    lax.fori_loop(0, blocks, proj_block, 0, unroll=True)
    for i in (0, blocks + 1):
        key_rows(i, dot(norm_rows(cond[i * LANES : (i + 1) * LANES, :].astype(F32)).astype(BF16), aw))

    for d in range(1, n_pair):
        ow_arrive(d).wait_recv()
    ow_cat[...] = jnp.zeros(ow_cat.shape, BF16)
    for h in range(n_pair):
        for j in range(4):
            ow_cat[h * LANES + 32 * j : h * LANES + 32 * j + 32, j * LANES : (j + 1) * LANES] = ow_all[h]

    lane32 = lax.broadcasted_iota(jnp.int32, (query_count, LANES), 1) // 32
    windows = atom_dev // query_count

    def score(w, carry):
        start = LANES + query_count * w + koff[w]
        window = keys[pl.ds(start, LANES), :].astype(BF16)
        window_keys[w] = window
        scores[w] = lax.dot_general(queries[w], window, NT, preferred_element_type=F32)
        return carry


    for w in range(windows):
        score(w, 0)

    for c in range(CHUNKS):
        for d in range(1, GROUP):
            receives(d, lambda: bias_arrive(c, d).wait_recv())
    for s in range(GROUP):
        whole = bias_all[s]
        high = whole.astype(BF16)
        bias_hi[s] = high
        bias_lo[s] = (whole - high.astype(F32)).astype(BF16)

    both = jnp.concatenate([bias_hi[...].reshape(group_tok, 2 * LANES), bias_lo[...].reshape(group_tok, 2 * LANES)], axis=0)
    for b in range(blocks):
        pick = onehot[first + b * LANES : first + (b + 1) * LANES, :group_tok]
        mine[b * LANES : (b + 1) * LANES, :] = dot(jnp.concatenate([pick, pick], axis=1), both)

    def soften(b, carry):
        rows = pl.ds(pl.multiple_of(b * LANES, LANES), LANES)
        raw = scores[pl.ds(4 * b, 4)]
        index = raw[:, query_count:].reshape(LANES, LANES).astype(jnp.int32)
        wrapped = index & (LANES - 1)
        low = jnp.take_along_axis(mine[rows, :LANES], wrapped, axis=1, mode="promise_in_bounds")
        high = jnp.take_along_axis(mine[rows, LANES:], wrapped, axis=1, mode="promise_in_bounds")
        value = raw[:, :query_count].reshape(LANES, LANES) * (1.0 / math.sqrt(32.0)) + jnp.where(
            index >= LANES, high, low
        )
        exponent = jnp.exp(value - jnp.max(value, axis=1, keepdims=True))
        weights[rows, :] = (exponent * (1.0 / jnp.sum(exponent, axis=1, keepdims=True))).astype(BF16)
        return carry


    def attend(b, carry):
        out = jnp.zeros((query_count, LANES), F32)
        for j in range(4):
            rows = pl.ds(pl.multiple_of(b * LANES + query_count * j, 32), query_count)
            gated = gate[rows, :] * dot(weights[rows, :], window_keys[4 * b + j])
            turned = gated if j == 2 else pltpu.roll(gated, (32 * j + 64) % LANES, 1)
            out = jnp.where(lane32 == j, turned, out)
        packed[p, pl.ds(pl.multiple_of(b * query_count, 32), query_count), :] = out.astype(BF16)
        return carry

    for b in range(blocks):
        soften(b, 0)
    for b in range(blocks):
        attend(b, 0)

    for b in range(blocks // SEND):
        for d in (2, 1, 3):
            gate_copy(b, d).start()

    for d in range(1, GROUP):
        tp_copy(d).wait_send()
        for c in range(CHUNKS):
            sends(d, lambda: bias_copy(c, d).wait_send())
    outside(lambda copy: copy.wait_send())
    to_right().wait_send()
    to_left().wait_send()
    for d in range(1, n_pair):
        ow_copy(d).wait_send()

    column_blocks = sums.shape[1]
    for k, (begin, end) in enumerate(PARTS):
        for b in range(blocks // SEND):
            for d in range(1, n_pair):
                gate_arrive(b, d).wait_recv()
        rows = slice(32 * begin, 32 * end)
        update = dot(packed[0, rows], ow_cat[0:LANES, :])
        for h in range(1, n_pair):
            update = update + dot(packed[h, rows], ow_cat[h * LANES : (h + 1) * LANES, :])
        for b in range(begin, end):
            for j in range(4):
                at = b * LANES + 32 * j
                value = cond[first + at : first + at + 32, :].astype(F32) + update[
                    32 * (b - begin) : 32 * (b - begin) + 32, j * LANES : (j + 1) * LANES
                ]
                atoms_bf[at : at + 32, :] = value.astype(BF16)
        span = slice(begin * LANES, end * LANES)
        atom_out[span, :] = atoms_bf[span, :]
        for c in range(column_blocks):
            per_atom = jnp.maximum(dot(atoms_bf[span, :], token_w[:, c * LANES : (c + 1) * LANES]), 0.0).astype(BF16)
            total = dot(onehot_t[:, span], per_atom)
            for t in range(GROUP):
                here = total[t * tok_dev : (t + 1) * tok_dev]
                if k > 0:
                    here = here + sums[t, c]
                sums[t, c] = here
                if k == len(PARTS) - 1:
                    sums_out[t, c] = here.astype(BF16)
    for d in (2, 1, 3):
        sends(d, lambda: sum_copy(0, d).start())
    for d in range(1, n_pair):
        for b in range(blocks // SEND):
            gate_copy(b, d).wait_send()
    eye = lax.broadcasted_iota(jnp.int32, (tok_dev, tok_dev), 0) == lax.broadcasted_iota(
        jnp.int32, (tok_dev, tok_dev), 1
    )
    count = jnp.sum(jnp.where(eye, counts[...].astype(F32), 0.0), axis=1, keepdims=True)
    inverse = 1.0 / count
    for d in range(1, GROUP):
        receives(d, lambda: sum_copy(0, d).wait_recv())
    for c in range(column_blocks):
        result = sums[r, c]
        for d in range(1, GROUP):
            result = result + sums_in[d, c].astype(F32)
        token_out[:, c * LANES : (c + 1) * LANES] = (result * inverse).astype(BF16)

    for d in range(1, GROUP):
        sends(d, lambda: sum_copy(0, d).wait_send())


def shards(
    trunk_single, atom_feature, pair_band, atom_token, token_counts, key_offsets,
    single_weight, attn_weight, bias_weight, out_weight, token_weight,
):
    n_dev = lax.axis_size("atoms")
    n_pair = lax.axis_size("pair")
    tok_dev, width = trunk_single.shape
    atom_dev = atom_feature.shape[0]
    blocks = atom_dev // LANES
    total_atoms = atom_token.shape[0]
    group_tok = GROUP * tok_dev
    ext = atom_dev + 2 * LANES
    vmem = pl.BlockSpec(memory_space=pltpu.VMEM)
    dma = pltpu.SemaphoreType.DMA
    return pl.pallas_call(
        functools.partial(kernel, (n_dev, n_pair, total_atoms)),
        out_shape=(
            jax.ShapeDtypeStruct((atom_dev, LANES), BF16),
            jax.ShapeDtypeStruct((tok_dev, width), BF16),
        ),
        in_specs=[
            pl.BlockSpec(memory_space=pl.ANY),
        ]
        * 11,
        out_specs=(vmem, vmem),
        scratch_shapes=[
            pltpu.VMEM(trunk_single.shape, BF16),
            pltpu.VMEM((ext, LANES), BF16),
            pltpu.VMEM((total_atoms // LANES, LANES), jnp.int32),
            pltpu.VMEM((1, tok_dev), jnp.int32),
            pltpu.SMEM(key_offsets.shape, jnp.int32),
            pltpu.VMEM(single_weight.shape, BF16),
            pltpu.VMEM((LANES, LANES), BF16),
            pltpu.VMEM((1, LANES), F32),
            pltpu.VMEM(token_weight.shape, BF16),
            dma((10,)),
            pltpu.VMEM(pair_band.shape, BF16),
            pltpu.VMEM((group_tok + LANES, LANES), BF16),
            pltpu.VMEM((GROUP, tok_dev, 2 * LANES), F32),
            pltpu.VMEM((ext, LANES), BF16),
            pltpu.VMEM((ext, LANES), F32),
            pltpu.VMEM((atom_dev // 32, 64, LANES), BF16),
            pltpu.VMEM((atom_dev, LANES), F32),
            pltpu.VMEM((ext, group_tok + LANES), BF16),
            pltpu.VMEM((group_tok, atom_dev), BF16),
            pltpu.VMEM((blocks + 2, LANES, LANES), jnp.int32),
            pltpu.VMEM((blocks + 2, LANES), jnp.int32),
            pltpu.VMEM((atom_dev, 2 * LANES), F32),
            pltpu.VMEM((atom_dev // 32, 64, LANES), F32),
            pltpu.VMEM((atom_dev, LANES), BF16),
            pltpu.VMEM((atom_dev // 32, LANES, LANES), BF16),
            pltpu.VMEM((n_pair, 32, LANES), BF16),
            pltpu.VMEM((n_pair * LANES, 4 * LANES), BF16),
            pltpu.VMEM((GROUP, tok_dev, 2 * LANES), BF16),
            pltpu.VMEM((GROUP, tok_dev, 2 * LANES), BF16),
            pltpu.VMEM((n_pair, atom_dev // 4, LANES), BF16),
            pltpu.VMEM((atom_dev, LANES), BF16),
            pltpu.VMEM((GROUP, width // LANES, tok_dev, LANES), F32),
            pltpu.VMEM((GROUP, width // LANES, tok_dev, LANES), BF16),
            pltpu.VMEM((GROUP, width // LANES, tok_dev, LANES), BF16),
            dma((CHUNKS,)),
            dma((GROUP,)), dma((GROUP,)),
            dma((n_pair,)), dma((n_pair,)),
            dma((CHUNKS, GROUP)), dma((CHUNKS, GROUP)),
            dma((2,)), dma((2,)),
            dma((blocks, n_pair)), dma((blocks, n_pair)),
            dma((width // LANES, GROUP)), dma((width // LANES, GROUP)),
        ],
        compiler_params=pltpu.CompilerParams(
            collective_id=0, has_side_effects=True, vmem_limit_bytes=48 * 1024 * 1024
        ),
        name="encoder",
    )(
        *(
            pltpu.with_memory_space_constraint(value, pltpu.HBM)
            for value in (
                trunk_single,
                atom_feature,
                pair_band,
                atom_token.reshape(total_atoms // LANES, LANES),
                token_counts.reshape(1, tok_dev),
                key_offsets,
                single_weight,
                attn_weight.reshape(attn_weight.shape[0], attn_weight.shape[2]),
                bias_weight.reshape(1, bias_weight.shape[0]),
                out_weight,
                token_weight,
            )
        )
    )


def solution(mesh):
    placed = (
        P("atoms", None),
        P("atoms", None),
        P("atoms", None, None),
        P(),
        P("atoms"),
        P("atoms"),
        P(),
        P(None, "pair", None),
        P(None, "pair"),
        P("pair", None),
        P(),
    )
    return jax.shard_map(
        shards,
        mesh=mesh,
        in_specs=placed,
        out_specs=(P("atoms", None), P("atoms", None)),
        check_vma=False,
    )
```
